128 devices in a mesh: frames: 128 (over y, x, z, core).
Axes of the slice: x: 4, y: 4, z: 4, core: 2. Of those that a mesh axis runs over, the one named last changes fastest.
Arguments:
- coords: bfloat16 [3, 131072, 256], P(None, 'frames'), may hold values from -20 to 20, as said below
Outputs:
- band: float32 [131072, 5, 1024], P('frames')
The draws below stay inside these ranges and needn't reach their ends.
Inputs may be any that keep to these rules, and one draw needn't show every extreme that they name: `coords`: frames are not centred.
All inputs are finite; a program needn't handle non-finite values.
Results may differ from the reference program's by a relative error of at most 0.0035.
Values may be sent and summed in bfloat16 or wider, within the bound.
A program may use at most 320 MiB of HBM per device.

```python
import math
import jax
import jax.numpy as jnp
from jax import lax

ATOMS = 256
FR_DEV = 1024
NEWTON = 8
BAND = 2
FRAMES = 131072
N_FRAMES = 128


def draw_coords(key, part):
    key = jax.random.fold_in(key, 7)
    keys = jax.random.split(key, 5)
    frame_scale = jnp.exp(jax.random.uniform(keys[0], (1, FRAMES, 1), jnp.float32, math.log(0.5), math.log(1.6)))
    atom_scale = jnp.exp(jax.random.uniform(keys[1], (1, 1, ATOMS), jnp.float32, math.log(0.5), math.log(1.6)))
    offset = jnp.clip(2.0 * jax.random.normal(keys[2], (3, FRAMES, 1), jnp.float32), -6.0, 6.0)
    structure = jnp.clip(jax.random.normal(keys[4], (3, FRAMES, ATOMS), jnp.float32), -4.0, 4.0)
    return (structure * frame_scale * atom_scale + offset).astype(jnp.bfloat16)


def setup_inputs(seed: int = 0) -> dict:
    key_of = jax.random.split(jax.random.key(seed), 2)
    coords = draw_coords(jax.random.fold_in(key_of[1], 71), 0)
    return {"coords": coords}


def centre(coords):
    values = coords.astype(jnp.float32)
    shifted = values - jnp.mean(values, axis=2, keepdims=True)
    return shifted.astype(jnp.bfloat16)


def frame_norms(centred):
    return jnp.sum(jnp.square(centred.astype(jnp.float32)), axis=(0, 2))


def deviation_tile(left, right, left_norms, right_norms):
    rows = left.shape[1]
    cols = right.shape[1]
    width = left.shape[2]
    cov = lax.dot_general(left.reshape(3 * rows, width), right.reshape(3 * cols, width),
                          (((1,), (1,)), ((), ())), preferred_element_type=jnp.float32)
    cov = cov.reshape(3, rows, 3, cols)
    entry = [[cov[k, :, l, :] for l in range(3)] for k in range(3)]
    squares = entry[0][0] * entry[0][0]
    for k in range(3):
        for l in range(3):
            if k + l > 0:
                squares = squares + entry[k][l] * entry[k][l]
    square_term = -2.0 * squares
    det_three = (entry[0][0] * (entry[1][1] * entry[2][2] - entry[1][2] * entry[2][1])
                 - entry[0][1] * (entry[1][0] * entry[2][2] - entry[1][2] * entry[2][0])
                 + entry[0][2] * (entry[1][0] * entry[2][1] - entry[1][1] * entry[2][0]))
    linear_term = -8.0 * det_three
    sxx, sxy, sxz = entry[0]
    syx, syy, syz = entry[1]
    szx, szy, szz = entry[2]
    horn = [[sxx + syy + szz, syz - szy, szx - sxz, sxy - syx],
            [syz - szy, sxx - syy - szz, sxy + syx, szx + sxz],
            [szx - sxz, sxy + syx, syy - sxx - szz, syz + szy],
            [sxy - syx, szx + sxz, syz + szy, szz - sxx - syy]]
    pairs = [(0, 1), (0, 2), (0, 3), (1, 2), (1, 3), (2, 3)]
    upper = [horn[0][p] * horn[1][q] - horn[1][p] * horn[0][q] for p, q in pairs]
    lower = [horn[2][p] * horn[3][q] - horn[3][p] * horn[2][q] for p, q in pairs]
    constant_term = (upper[0] * lower[5] - upper[1] * lower[4] + upper[2] * lower[3]
                     + upper[3] * lower[2] - upper[4] * lower[1] + upper[5] * lower[0])
    pair_norms = left_norms[:, None] + right_norms[None, :]
    top = 0.5 * pair_norms
    for step in range(NEWTON):
        square = top * top
        value = ((square + square_term) * top + linear_term) * top + constant_term
        slope = (4.0 * square + 2.0 * square_term) * top + linear_term
        top = top - value / slope
    return (pair_norms - 2.0 * top) / width


def reference(coords):
    centred = centre(coords)
    norms = frame_norms(centred)
    blocks = jnp.transpose(centred.reshape(3, N_FRAMES, FR_DEV, ATOMS), (1, 0, 2, 3))
    block_norms = norms.reshape(N_FRAMES, FR_DEV)

    def row_tiles(index):
        mine = blocks[index]
        tiles = []
        for step in range(BAND + 1):
            other = (index + step) % N_FRAMES
            tiles.append(deviation_tile(mine, blocks[other], block_norms[index], block_norms[other]))
        return jnp.stack(tiles, axis=0)

    forward = lax.map(row_tiles, jnp.arange(N_FRAMES, dtype=jnp.int32))
    pieces = []
    for offset in range(2 * BAND + 1):
        step = offset - BAND
        if step >= 0:
            pieces.append(forward[:, step])
        else:
            pieces.append(jnp.swapaxes(jnp.roll(forward[:, -step], -step, axis=0), 1, 2))
    band = jnp.stack(pieces, axis=2)
    return band.reshape(FRAMES, 2 * BAND + 1, FR_DEV)
```

```python
import functools

import jax
import jax.numpy as jnp
from jax import lax
from jax.experimental import pallas as pl
from jax.experimental.pallas import tpu as pltpu
from jax.sharding import PartitionSpec as P

NEWTON = 8
FR = 1024
ATOMS = 256
ROWS = 128
COLS = 256
HALF = FR // 2
VMEM = pl.BlockSpec(memory_space=pltpu.VMEM)
ANY = pl.BlockSpec(memory_space=pl.ANY)
PARAMS = pltpu.CompilerParams(vmem_limit_bytes=40 << 20)


def aligned(index, size):
    return pl.ds(pl.multiple_of(index, size), size)


def centre_kernel(x_ref, c_ref, n_ref):
    total = None
    for k in range(3):
        values = x_ref[k].astype(jnp.float32)
        mean = jnp.sum(values, axis=1, keepdims=True) * (1.0 / ATOMS)
        centred = (values - mean).astype(jnp.bfloat16)
        c_ref[k] = centred
        back = centred.astype(jnp.float32)
        square = back * back
        total = square if total is None else total + square
    norms = 0.5 * jnp.sum(total, axis=1, keepdims=True)
    n_ref[...] = jnp.broadcast_to(norms, n_ref.shape)


def centre(coords):
    rows = 256
    return pl.pallas_call(
        centre_kernel,
        grid=(FR // rows,),
        in_specs=[pl.BlockSpec((3, rows, ATOMS), lambda i: (0, i, 0))],
        out_specs=[
            pl.BlockSpec((3, rows, ATOMS), lambda i: (0, i, 0)),
            pl.BlockSpec((rows, 128), lambda i: (i, 0)),
        ],
        out_shape=[
            jax.ShapeDtypeStruct((3, FR, ATOMS), jnp.bfloat16),
            jax.ShapeDtypeStruct((FR, 128), jnp.float32),
        ],
        name="centre",
    )(coords)


def row_norms(b_ref, first, count, rn_ref):
    @pl.loop(0, count // 128)
    def _(i):
        frames = aligned(first + i * 128, 128)
        total = None
        for k in range(3):
            values = b_ref[k, frames, :].astype(jnp.float32)
            total = values * values if total is None else total + values * values
        norms = 0.5 * jnp.sum(total, axis=1, keepdims=True)
        square = jnp.broadcast_to(norms, (128, 128)).T
        rn_ref[:, frames] = square[0:8, :]


def invariants(entry):
    (a, b, c), (d, f, g), (h, i, j) = entry
    first = a * a + b * b + c * c
    others = (d * d + f * f + g * g) + (h * h + i * i + j * j)
    p = f * j - g * i
    q = g * h - d * j
    r = d * i - f * h
    det = a * p + b * q + c * r
    one = a * d + b * f + c * g
    two = a * h + b * i + c * j
    minors = (first * others - one * one - two * two) + (p * p + q * q + r * r)
    return first + others, det + det, minors


def deviations(entry, left, right):
    n, f, m = invariants(entry)
    start = left + right
    top = start
    for _ in range(NEWTON):
        h = top * top - n
        top = ((h * 0.75 + n) * h + m) * pltpu.reciprocal(top * h - f, approx=True)
    return (start - top) * (2.0 / ATOMS)


def covariance(a_ref, b_ref, row, col, cov_ref):
    left = a_ref[:, aligned(row, ROWS), :].reshape(3 * ROWS, ATOMS)
    for k in range(3):
        right = b_ref[k, aligned(col, COLS), :]
        block = lax.dot_general(
            left, right, (((1,), (1,)), ((), ())), preferred_element_type=jnp.float32
        )
        cov_ref[:, k] = block.reshape(3, ROWS, COLS)


def step_values(cov_ref, ln_ref, rn_ref, row, col, emit):
    step = 16
    for r in range(0, ROWS, step):
        entry = [[cov_ref[k, l, r : r + step, :] for l in range(3)] for k in range(3)]
        left = ln_ref[pl.ds(pl.multiple_of(row + r, step), step), :]
        left = jnp.concatenate([left] * (COLS // 128), axis=1)
        right = rn_ref[:, aligned(col, COLS)]
        right = jnp.concatenate([right] * (step // 8), axis=0)
        emit(r, step, deviations(entry, left, right))


def run_steps(total, place, a_ref, b_ref, ln_ref, rn_ref, cov0, cov1, emit, after):
    covariance(a_ref, b_ref, *place(0), cov0)

    @pl.loop(0, total // 2)
    def _(i):
        even, odd = 2 * i, 2 * i + 1
        covariance(a_ref, b_ref, *place(odd), cov1)
        step_values(cov0, ln_ref, rn_ref, *place(even), functools.partial(emit, even))
        after(even)
        covariance(a_ref, b_ref, *place(jnp.minimum(odd + 1, total - 1)), cov0)
        step_values(cov1, ln_ref, rn_ref, *place(odd), functools.partial(emit, odd))
        after(odd)


def encode(values):
    square = values * values
    return (square * square).astype(jnp.bfloat16)


def diagonal_kernel(a_ref, ln_ref, out_ref, tile, rn, cov0, cov1, sem):
    row_norms(a_ref, 0, FR, rn)
    per = COLS // ROWS

    def place(s):
        col = 0
        for c in range(1, FR // COLS):
            col = col + jnp.where(s >= per * c * (c + 1) // 2, 1, 0)
        row = s - per * col * (col + 1) // 2
        return row * ROWS, col * COLS

    def emit(s, r, step, values):
        row, col = place(s)
        tile[pl.ds(pl.multiple_of(row + r, step), step), aligned(col, COLS)] = values

    def after(s):
        row, col = place(s)
        rows, cols = aligned(row, ROWS), aligned(col, COLS)

        @pl.when(row < col)
        def _():
            tile[cols, rows] = tile[rows, cols].T

    total = per * (FR // COLS) * (FR // COLS + 1) // 2
    run_steps(total, place, a_ref, a_ref, ln_ref, rn, cov0, cov1, emit, after)
    copy = pltpu.make_async_copy(tile, out_ref.at[2], sem)
    copy.start()
    copy.wait()


def diagonal(centred, norms):
    return pl.pallas_call(
        diagonal_kernel,
        in_specs=[VMEM, VMEM],
        out_specs=ANY,
        out_shape=jax.ShapeDtypeStruct((5, FR, FR), jnp.float32),
        scratch_shapes=[
            pltpu.VMEM((FR, FR), jnp.float32),
            pltpu.VMEM((8, FR), jnp.float32),
            pltpu.VMEM((3, 3, ROWS, COLS), jnp.float32),
            pltpu.VMEM((3, 3, ROWS, COLS), jnp.float32),
            pltpu.SemaphoreType.DMA,
        ],
        compiler_params=PARAMS,
        cost_estimate=pl.CostEstimate(
            flops=9 * FR * FR * ATOMS, bytes_accessed=6 << 20, transcendentals=0
        ),
        name="diagonal",
    )(centred, norms)


def far_kernel(first, count, a_ref, b_ref, ln_ref, _, out_ref, y_ref, tile, rn, cov0, cov1, sem):
    parity = lax.rem(lax.axis_index("frames"), 2)
    slot = 4 * (1 - parity)
    row_norms(b_ref, first, count, rn)
    per = FR // ROWS

    def place(s):
        return (s % per) * ROWS, first + (s // per) * COLS

    def emit(s, r, step, values):
        row, col = place(s)
        tile[pl.ds(pl.multiple_of(row + r, step), step), aligned(col - first, COLS)] = values

    def after(s):
        row, col = place(s)
        rows, cols = aligned(row, ROWS), aligned(col - first, COLS)
        y_ref[cols, rows] = encode(tile[rows, cols]).T
        pltpu.make_async_copy(
            tile.at[rows, cols], out_ref.at[slot, rows, aligned(col, COLS)], sem
        ).start()

    total = per * (count // COLS)
    run_steps(total, place, a_ref, b_ref, ln_ref, rn, cov0, cov1, emit, after)
    pltpu.make_async_copy(tile, out_ref.at[slot, :, pl.ds(first, count)], sem).wait()


def far_part(centred, other, norms, out, first, count):
    return pl.pallas_call(
        functools.partial(far_kernel, first, count),
        in_specs=[VMEM, VMEM, VMEM, ANY],
        out_specs=[ANY, VMEM],
        out_shape=[
            jax.ShapeDtypeStruct((5, FR, FR), jnp.float32),
            jax.ShapeDtypeStruct((count, FR), jnp.bfloat16),
        ],
        input_output_aliases={3: 0},
        scratch_shapes=[
            pltpu.VMEM((FR, count), jnp.float32),
            pltpu.VMEM((8, FR), jnp.float32),
            pltpu.VMEM((3, 3, ROWS, COLS), jnp.float32),
            pltpu.VMEM((3, 3, ROWS, COLS), jnp.float32),
            pltpu.SemaphoreType.DMA,
        ],
        compiler_params=PARAMS,
        cost_estimate=pl.CostEstimate(
            flops=18 * FR * count * ATOMS, bytes_accessed=6 << 20, transcendentals=0
        ),
        name="far",
    )(centred, other, norms, out)


def quarters_kernel(mate, a_ref, b_ref, ln_ref, _, out_ref, y_ref, tile, rn, cov0, cov1, sem):
    parity = lax.rem(lax.axis_index("frames"), 2)
    if mate:
        slot, flip = 3 - 2 * parity, parity
    else:
        slot, flip = 1 + 2 * parity, 1 - parity
    row_norms(b_ref, 0, FR, rn)
    per_row, per_col = HALF // ROWS, HALF // COLS
    per = per_row * per_col

    def place(s):
        half = s // per
        other = half + flip - 2 * half * flip
        inner = s % per
        row = half * HALF + (inner % per_row) * ROWS
        return row, other * HALF + (inner // per_row) * COLS

    def local(s):
        half, inner = s // per, s % per
        return half, (inner % per_row) * ROWS, (inner // per_row) * COLS

    def emit(s, r, step, values):
        half, row, col = local(s)
        tile[half, pl.ds(pl.multiple_of(row + r, step), step), aligned(col, COLS)] = values

    def after(s):
        half, row, col = local(s)
        rows, cols = aligned(row, ROWS), aligned(col, COLS)
        y_ref[half, cols, rows] = encode(tile[half, rows, cols]).T
        row, col = place(s)
        pltpu.make_async_copy(
            tile.at[half, rows, cols],
            out_ref.at[slot, aligned(row, ROWS), aligned(col, COLS)],
            sem,
        ).start()

    run_steps(2 * per, place, a_ref, b_ref, ln_ref, rn, cov0, cov1, emit, after)
    for half in range(2):
        pltpu.make_async_copy(
            tile.at[half], out_ref.at[slot, pl.ds(0, HALF), pl.ds(0, HALF)], sem
        ).wait()


def quarters(centred, other, norms, out, mate):
    return pl.pallas_call(
        functools.partial(quarters_kernel, mate),
        in_specs=[VMEM, VMEM, VMEM, ANY],
        out_specs=[ANY, VMEM],
        out_shape=[
            jax.ShapeDtypeStruct((5, FR, FR), jnp.float32),
            jax.ShapeDtypeStruct((2, HALF, HALF), jnp.bfloat16),
        ],
        input_output_aliases={3: 0},
        scratch_shapes=[
            pltpu.VMEM((2, HALF, HALF), jnp.float32),
            pltpu.VMEM((8, FR), jnp.float32),
            pltpu.VMEM((3, 3, ROWS, COLS), jnp.float32),
            pltpu.VMEM((3, 3, ROWS, COLS), jnp.float32),
            pltpu.SemaphoreType.DMA,
        ],
        compiler_params=PARAMS,
        cost_estimate=pl.CostEstimate(
            flops=9 * FR * FR * ATOMS, bytes_accessed=6 << 20, transcendentals=0
        ),
        name="mate" if mate else "near",
    )(centred, other, norms, out)


def decode(values):
    return lax.rsqrt(lax.rsqrt(values.astype(jnp.float32)))


def received_kernel(far0, far1, near, mate, _, out_ref, far_tile, near_tile, mate_tile, sem):
    parity = lax.rem(lax.axis_index("frames"), 2)
    copies = []
    for i, (ref, rows) in enumerate(((far0, pl.ds(0, HALF)), (far1, pl.ds(HALF, HALF)))):
        far_tile[rows, :] = decode(ref[...])
        copies.append(pltpu.make_async_copy(
            far_tile.at[rows], out_ref.at[4 * parity, rows], sem.at[i]
        ))
        copies[-1].start()
    for i, (ref, tile, slot, flip) in enumerate(
        ((near, near_tile, 1 + 2 * parity, parity), (mate, mate_tile, 3 - 2 * parity, 1 - parity))
    ):
        for half in range(2):
            tile[half] = decode(ref[half])
            own = half + flip - 2 * half * flip
            copies.append(pltpu.make_async_copy(
                tile.at[half],
                out_ref.at[slot, aligned(own * HALF, HALF), pl.ds(half * HALF, HALF)],
                sem.at[2 + 2 * i + half],
            ))
            copies[-1].start()
    for copy in copies:
        copy.wait()


def received(far0, far1, near, mate, out):
    return pl.pallas_call(
        received_kernel,
        in_specs=[VMEM, VMEM, VMEM, VMEM, ANY],
        out_specs=ANY,
        out_shape=jax.ShapeDtypeStruct((5, FR, FR), jnp.float32),
        input_output_aliases={4: 0},
        scratch_shapes=[
            pltpu.VMEM((FR, FR), jnp.float32),
            pltpu.VMEM((2, HALF, HALF), jnp.float32),
            pltpu.VMEM((2, HALF, HALF), jnp.float32),
            pltpu.SemaphoreType.DMA((6,)),
        ],
        compiler_params=PARAMS,
        name="received",
    )(far0, far1, near, mate, out)


def on_device(coords):
    count = lax.axis_size("frames")
    reach = [2 if s % 2 == 0 else -2 for s in range(count)]
    fetch_far = [((s + reach[s]) % count, s) for s in range(count)]
    send_far = [(s, (s + reach[s]) % count) for s in range(count)]
    send_near = [(s, (s - 1 if s % 2 == 0 else s + 1) % count) for s in range(count)]
    swap = [(s, s ^ 1) for s in range(count)]
    move = functools.partial(lax.ppermute, axis_name="frames")

    centred, norms = centre(coords)
    far = move(centred, perm=fetch_far)
    mate = move(centred, perm=swap)
    out = diagonal(centred, norms)
    far, out = lax.optimization_barrier((far, out))
    near = move(far, perm=swap)
    out, far0 = far_part(centred, far, norms, out, 0, HALF)
    far0 = move(far0, perm=send_far)
    out, far1 = far_part(centred, far, norms, out, HALF, HALF)
    far1 = move(far1, perm=send_far)
    out, near_y = quarters(centred, near, norms, out, False)
    near_y = move(near_y, perm=send_near)
    out, mate_y = quarters(centred, mate, norms, out, True)
    mate_y = move(mate_y, perm=swap)
    out = received(far0, far1, near_y, mate_y, out)
    return jnp.transpose(out, (1, 0, 2))


def solution(mesh):
    return jax.shard_map(
        on_device,
        mesh=mesh,
        in_specs=(P(None, "frames", None),),
        out_specs=P("frames", None, None),
        check_vma=False,
    )
```

```python
import functools

import jax
import jax.numpy as jnp
from jax import lax
from jax.experimental import pallas as pl
from jax.experimental.pallas import tpu as pltpu
from jax.sharding import PartitionSpec as P

NEWTON = 8
FR = 1024
ATOMS = 256
ROWS = 128
COLS = 256
STEP = 16
HALF = FR // 2
VMEM = pl.BlockSpec(memory_space=pltpu.VMEM)
ANY = pl.BlockSpec(memory_space=pl.ANY)
PARAMS = pltpu.CompilerParams(vmem_limit_bytes=32 << 20)


def aligned(index, size):
    return pl.ds(pl.multiple_of(index, size), size)


def centre_kernel(x_ref, c_ref, low_ref, high_ref, n_ref):
    for part, ref in enumerate((low_ref, high_ref)):

        @pl.loop(0, HALF // ROWS)
        def _(i):
            inner = aligned(i * ROWS, ROWS)
            rows = aligned(part * HALF + i * ROWS, ROWS)
            total = None
            for k in range(3):
                values = x_ref[k, rows, :].astype(jnp.float32)
                mean = jnp.sum(values, axis=1, keepdims=True) * (1.0 / ATOMS)
                centred = (values - mean).astype(jnp.bfloat16)
                c_ref[k, rows, :] = centred
                ref[k, inner, :] = centred
                back = centred.astype(jnp.float32)
                square = back * back
                total = square if total is None else total + square
            norms = 0.5 * jnp.sum(total, axis=1, keepdims=True)
            n_ref[rows, :] = jnp.broadcast_to(norms, (ROWS, 128))


def centre(coords):
    return pl.pallas_call(
        centre_kernel,
        in_specs=[VMEM],
        out_specs=[VMEM] * 4,
        out_shape=[
            jax.ShapeDtypeStruct((3, FR, ATOMS), jnp.bfloat16),
            jax.ShapeDtypeStruct((3, HALF, ATOMS), jnp.bfloat16),
            jax.ShapeDtypeStruct((3, HALF, ATOMS), jnp.bfloat16),
            jax.ShapeDtypeStruct((FR, 128), jnp.float32),
        ],
        compiler_params=pltpu.CompilerParams(vmem_limit_bytes=16 << 20),
        name="centre",
    )(coords)


def row_norms(b_ref, rn_ref):
    @pl.loop(0, b_ref.shape[1] // 128)
    def _(i):
        frames = aligned(i * 128, 128)
        total = None
        for k in range(3):
            values = b_ref[k, frames, :].astype(jnp.float32)
            total = values * values if total is None else total + values * values
        norms = 0.5 * jnp.sum(total, axis=1, keepdims=True)
        square = jnp.broadcast_to(norms, (128, 128)).T
        rn_ref[:, frames] = square[0:8, :]


def invariants(entry):
    (a, b, c), (d, f, g), (h, i, j) = entry
    first = a * a + b * b + c * c
    others = (d * d + f * f + g * g) + (h * h + i * i + j * j)
    p = f * j - g * i
    q = g * h - d * j
    r = d * i - f * h
    det = a * p + b * q + c * r
    one = a * d + b * f + c * g
    two = a * h + b * i + c * j
    minors = (first * others - one * one - two * two) + (p * p + q * q + r * r)
    return first + others, det + det, minors


def deviations(entry, left, right):
    n, f, m = invariants(entry)
    start = left + right
    top = start
    for _ in range(NEWTON):
        h = top * top - n
        top = ((h * 0.75 + n) * h + m) * pltpu.reciprocal(top * h - f, approx=True)
    return (start - top) * (2.0 / ATOMS)


def covariance_pieces(a_ref, b_ref, row, col, cov_ref):
    left = a_ref[:, aligned(row, ROWS), :].reshape(3 * ROWS, ATOMS)
    for k in range(3):
        right = b_ref[k, aligned(col, COLS), :]
        block = lax.dot_general(
            left, right, (((1,), (1,)), ((), ())), preferred_element_type=jnp.float32
        )
        cov_ref[:, k] = block.reshape(3, ROWS, COLS)
        yield


def value_pieces(cov_ref, ln_ref, rn_ref, row, col, emit):
    for r in range(0, ROWS, STEP):
        entry = [[cov_ref[k, l, r : r + STEP, :] for l in range(3)] for k in range(3)]
        left = ln_ref[aligned(row + r, STEP), :]
        left = jnp.concatenate([left] * (COLS // 128), axis=1)
        right = rn_ref[:, aligned(col, COLS)]
        right = jnp.concatenate([right] * (STEP // 8), axis=0)
        emit(r, deviations(entry, left, right))
        yield


def run_steps(total, place, a_ref, b_ref, ln_ref, rn_ref, cov0, cov1, old0, old1, keep, turn, before):
    for _ in covariance_pieces(a_ref, b_ref, *place(0), cov0):
        pass

    def step(s, cov, cov_next, old, old_last):
        row, col = place(jnp.minimum(s + 1, total - 1))
        products = covariance_pieces(a_ref, b_ref, row, col, cov_next)
        row, col = place(s)
        values = value_pieces(cov, ln_ref, rn_ref, row, col, functools.partial(keep, s, old))
        for count, _ in enumerate(values):
            if count in (0, 2, 4):
                next(products)
        turn(jnp.maximum(s - 1, 0), old_last)

    @pl.loop(0, total)
    def _(s):
        before(s)

        @pl.when((s & 1) == 0)
        def _():
            step(s, cov0, cov1, old0, old1)

        @pl.when((s & 1) == 1)
        def _():
            step(s, cov1, cov0, old1, old0)

    turn(total - 1, old1 if total % 2 == 0 else old0)
    before(total)
    before(total + 1)


def encode(values):
    square = values * values
    return (square * square).astype(jnp.bfloat16)


def step_scratch(kind):
    return [
        pltpu.VMEM((3, 3, ROWS, COLS), jnp.float32),
        pltpu.VMEM((3, 3, ROWS, COLS), jnp.float32),
        pltpu.VMEM((ROWS, COLS), kind),
        pltpu.VMEM((ROWS, COLS), kind),
    ]


def diagonal_kernel(first, last, a_ref, ln_ref, *refs):
    out_ref, tile, mirror, rn, cov0, cov1, old0, old1, sem = refs[-9:]
    row_norms(a_ref, rn)
    per = COLS // ROWS
    starts = [per * c * (c + 1) // 2 for c in range(FR // COLS + 1)]

    def place(s):
        s = s + starts[first]
        col = sum(jnp.where(s >= start, 1, 0) for start in starts[1:last])
        row = s - per * (col * (col + 1) // 2)
        return row * ROWS, col * COLS

    def keep(s, old, r, values):
        row, col = place(s)
        tile[aligned(row + r, STEP), aligned(col, COLS)] = values
        old[r : r + STEP, :] = values

    def turn(s, old):
        row, col = place(s)
        mirror[aligned(col, COLS), aligned(row, ROWS)] = old[...].T

    def copies(c):
        cols = pl.ds(c * COLS, COLS)
        yield tile, pl.ds(0, (c + 1) * COLS), cols
        if c > 0:
            yield mirror, cols, pl.ds(0, c * COLS)

    def each_copy(c, act):
        for source, rows, cols in copies(c):
            act(pltpu.make_async_copy(source.at[rows, cols], out_ref.at[2, rows, cols], sem.at[c]))

    def before(s):
        for c in range(first, last):
            if isinstance(s, int):
                if s == starts[c + 1] - starts[first] + 1:
                    each_copy(c, lambda copy: copy.start())
            elif c + 1 < last:

                @pl.when(s == starts[c + 1] - starts[first] + 1)
                def _():
                    each_copy(c, lambda copy: copy.start())

    total = starts[last] - starts[first]
    run_steps(
        total, place, a_ref, a_ref, ln_ref, rn, cov0, cov1, old0, old1, keep, turn, before
    )
    for c in range(first, last):
        each_copy(c, lambda copy: copy.wait())


def diagonal(centred, norms, out, first, last):
    given = () if out is None else (out,)
    return pl.pallas_call(
        functools.partial(diagonal_kernel, first, last),
        in_specs=[VMEM, VMEM] + [ANY] * len(given),
        out_specs=ANY,
        out_shape=jax.ShapeDtypeStruct((5, FR, FR), jnp.float32),
        input_output_aliases={2: 0} if given else {},
        scratch_shapes=[
            pltpu.VMEM((FR, FR), jnp.float32),
            pltpu.VMEM((FR, FR), jnp.float32),
            pltpu.VMEM((8, FR), jnp.float32),
            *step_scratch(jnp.float32),
            pltpu.SemaphoreType.DMA((FR // COLS,)),
        ],
        compiler_params=PARAMS,
        cost_estimate=pl.CostEstimate(
            flops=9 * FR * FR * ATOMS, bytes_accessed=6 << 20, transcendentals=0
        ),
        name="diagonal",
    )(centred, norms, *given)


def far_kernel(part, a_ref, b_ref, ln_ref, _, out_ref, y_ref, tile, rn, cov0, cov1, old0, old1, sem):
    parity = lax.rem(lax.axis_index("frames"), 2)
    slot = 4 * (1 - parity)
    row_norms(b_ref, rn)
    per = FR // ROWS
    total = per * (HALF // COLS)

    def place(s):
        return (s & (per - 1)) * ROWS, (s // per) * COLS

    def keep(s, old, r, values):
        row, col = place(s)
        tile[aligned(row + r, STEP), aligned(col, COLS)] = values
        old[r : r + STEP, :] = encode(values)

    def turn(s, old):
        row, col = place(s)
        y_ref[aligned(col, COLS), aligned(row, ROWS)] = old[...].T

    def column_copy(c):
        cols = pl.ds(c * COLS, COLS)
        target = out_ref.at[slot, :, pl.ds(part * HALF + c * COLS, COLS)]
        return pltpu.make_async_copy(tile.at[:, cols], target, sem.at[c])

    def before(s):
        for c in range(HALF // COLS):
            if isinstance(s, int):
                if s == (c + 1) * per:
                    column_copy(c).start()
            elif (c + 1) * per < total:

                @pl.when(s == (c + 1) * per)
                def _():
                    column_copy(c).start()

    run_steps(
        total, place, a_ref, b_ref, ln_ref, rn, cov0, cov1, old0, old1, keep, turn, before
    )
    for c in range(HALF // COLS):
        column_copy(c).wait()


def far_part(centred, other, norms, out, part):
    return pl.pallas_call(
        functools.partial(far_kernel, part),
        in_specs=[VMEM, VMEM, VMEM, ANY],
        out_specs=[ANY, VMEM],
        out_shape=[
            jax.ShapeDtypeStruct((5, FR, FR), jnp.float32),
            jax.ShapeDtypeStruct((HALF, FR), jnp.bfloat16),
        ],
        input_output_aliases={3: 0},
        scratch_shapes=[
            pltpu.VMEM((FR, HALF), jnp.float32),
            pltpu.VMEM((8, HALF), jnp.float32),
            *step_scratch(jnp.bfloat16),
            pltpu.SemaphoreType.DMA((HALF // COLS,)),
        ],
        compiler_params=PARAMS,
        cost_estimate=pl.CostEstimate(
            flops=9 * FR * FR * ATOMS, bytes_accessed=6 << 20, transcendentals=0
        ),
        name="far",
    )(centred, other, norms, out)


def quarters_kernel(mate, a_ref, ln_ref, *refs):
    *others, _, out_ref, y_ref, b_ref, tile, rn, cov0, cov1, old0, old1, b_sem, sem = refs
    parity = lax.rem(lax.axis_index("frames"), 2)
    if mate:
        slot, flip = 3 - 2 * parity, parity
    else:
        slot, flip = 1 + 2 * parity, 1 - parity
    size = FR // len(others)
    loads = [
        pltpu.make_async_copy(ref, b_ref.at[:, pl.ds(i * size, size)], b_sem.at[i])
        for i, ref in enumerate(others)
    ]
    for load in loads:
        load.start()
    for load in loads:
        load.wait()
    row_norms(b_ref, rn)
    per_row, per_col = HALF // ROWS, HALF // COLS
    per = per_row * per_col

    def local(s):
        inner = s & (per - 1)
        return s // per, (inner & (per_row - 1)) * ROWS, (inner // per_row) * COLS

    def place(s):
        half, row, col = local(s)
        other = half + flip - 2 * half * flip
        return half * HALF + row, other * HALF + col

    def keep(s, old, r, values):
        half, row, col = local(s)
        tile[half, aligned(row + r, STEP), aligned(col, COLS)] = values
        old[r : r + STEP, :] = encode(values)

    def turn(s, old):
        half, row, col = local(s)
        y_ref[half, aligned(col, COLS), aligned(row, ROWS)] = old[...].T

    def half_copy(half):
        other = half + flip - 2 * half * flip
        target = out_ref.at[slot, pl.ds(half * HALF, HALF), aligned(other * HALF, HALF)]
        return pltpu.make_async_copy(tile.at[half], target, sem.at[half])

    def before(s):
        if isinstance(s, int):
            if s == 2 * per:
                half_copy(1).start()
        else:

            @pl.when(s == per)
            def _():
                half_copy(0).start()

    run_steps(
        2 * per, place, a_ref, b_ref, ln_ref, rn, cov0, cov1, old0, old1, keep, turn, before
    )
    for half in range(2):
        half_copy(half).wait()


def quarters(centred, others, norms, out, mate):
    return pl.pallas_call(
        functools.partial(quarters_kernel, mate),
        in_specs=[VMEM, VMEM] + [ANY] * len(others) + [ANY],
        out_specs=[ANY, VMEM],
        out_shape=[
            jax.ShapeDtypeStruct((5, FR, FR), jnp.float32),
            jax.ShapeDtypeStruct((2, HALF, HALF), jnp.bfloat16),
        ],
        input_output_aliases={2 + len(others): 0},
        scratch_shapes=[
            pltpu.VMEM((3, FR, ATOMS), jnp.bfloat16),
            pltpu.VMEM((2, HALF, HALF), jnp.float32),
            pltpu.VMEM((8, FR), jnp.float32),
            *step_scratch(jnp.bfloat16),
            pltpu.SemaphoreType.DMA((len(others),)),
            pltpu.SemaphoreType.DMA((2,)),
        ],
        compiler_params=PARAMS,
        cost_estimate=pl.CostEstimate(
            flops=9 * FR * FR * ATOMS, bytes_accessed=6 << 20, transcendentals=0
        ),
        name="mate" if mate else "near",
    )(centred, norms, *others, out)


def decode(values):
    return lax.rsqrt(lax.rsqrt(values.astype(jnp.float32)))


def received_kernel(far0, far1, near, mate, _, out_ref, far_tile, near_tile, mate_tile, sem):
    parity = lax.rem(lax.axis_index("frames"), 2)
    copies = []
    for i, (ref, rows) in enumerate(((far0, pl.ds(0, HALF)), (far1, pl.ds(HALF, HALF)))):
        far_tile[rows, :] = decode(ref[...])
        copies.append(pltpu.make_async_copy(
            far_tile.at[rows], out_ref.at[4 * parity, rows], sem.at[i]
        ))
        copies[-1].start()
    for i, (ref, tile, slot, flip) in enumerate(
        ((near, near_tile, 1 + 2 * parity, parity), (mate, mate_tile, 3 - 2 * parity, 1 - parity))
    ):
        for half in range(2):
            tile[half] = decode(ref[half])
            own = half + flip - 2 * half * flip
            copies.append(pltpu.make_async_copy(
                tile.at[half],
                out_ref.at[slot, aligned(own * HALF, HALF), pl.ds(half * HALF, HALF)],
                sem.at[2 + 2 * i + half],
            ))
            copies[-1].start()
    for copy in copies:
        copy.wait()


def received(far0, far1, near, mate, out):
    return pl.pallas_call(
        received_kernel,
        in_specs=[VMEM, VMEM, VMEM, VMEM, ANY],
        out_specs=ANY,
        out_shape=jax.ShapeDtypeStruct((5, FR, FR), jnp.float32),
        input_output_aliases={4: 0},
        scratch_shapes=[
            pltpu.VMEM((FR, FR), jnp.float32),
            pltpu.VMEM((2, HALF, HALF), jnp.float32),
            pltpu.VMEM((2, HALF, HALF), jnp.float32),
            pltpu.SemaphoreType.DMA((6,)),
        ],
        compiler_params=PARAMS,
        name="received",
    )(far0, far1, near, mate, out)


def on_device(coords):
    count = lax.axis_size("frames")
    reach = [2 if s % 2 == 0 else -2 for s in range(count)]
    fetch_far = [((s + reach[s]) % count, s) for s in range(count)]
    send_far = [(s, (s + reach[s]) % count) for s in range(count)]
    send_near = [(s, (s - 1 if s % 2 == 0 else s + 1) % count) for s in range(count)]
    swap = [(s, s ^ 1) for s in range(count)]
    move = functools.partial(lax.ppermute, axis_name="frames")

    centred, low, high, norms = centre(coords)
    far_low = move(low, perm=fetch_far)
    far_high = move(high, perm=fetch_far)
    mate = move(centred, perm=swap)
    blocks = FR // COLS
    out = diagonal(centred, norms, None, 0, blocks - 1)
    far_low, out = lax.optimization_barrier((far_low, out))
    near_low = move(far_low, perm=swap)
    out, far0 = far_part(centred, far_low, norms, out, 0)
    far_high, out, far0 = lax.optimization_barrier((far_high, out, far0))
    near_high = move(far_high, perm=swap)
    far0 = move(far0, perm=send_far)
    out, far1 = far_part(centred, far_high, norms, out, 1)
    far1 = move(far1, perm=send_far)
    out, near_y = quarters(centred, (near_low, near_high), norms, out, False)
    near_y = move(near_y, perm=send_near)
    out, mate_y = quarters(centred, (mate,), norms, out, True)
    mate_y = move(mate_y, perm=swap)
    out = diagonal(centred, norms, out, blocks - 1, blocks)
    out = received(far0, far1, near_y, mate_y, out)
    return jnp.transpose(out, (1, 0, 2))


def solution(mesh):
    return jax.shard_map(
        on_device,
        mesh=mesh,
        in_specs=(P(None, "frames", None),),
        out_specs=P("frames", None, None),
        check_vma=False,
    )
```

```python
import functools

import jax
import jax.numpy as jnp
from jax import lax
from jax.experimental import pallas as pl
from jax.experimental.pallas import tpu as pltpu
from jax.sharding import PartitionSpec as P

NEWTON = 8
FR = 1024
ATOMS = 256
ROWS = 128
COLS = 256
STEP = 16
HALF = FR // 2
VMEM = pl.BlockSpec(memory_space=pltpu.VMEM)
ANY = pl.BlockSpec(memory_space=pl.ANY)
PARAMS = pltpu.CompilerParams(vmem_limit_bytes=8 << 20)
COST = pl.CostEstimate(flops=9 * FR * FR * ATOMS, bytes_accessed=6 << 20, transcendentals=0)


def aligned(index, size):
    return pl.ds(pl.multiple_of(index, size), size)


def centre_kernel(x_ref, c_ref, low_ref, high_ref, n_ref):
    for part, ref in enumerate((low_ref, high_ref)):

        @pl.loop(0, HALF // ROWS)
        def _(i):
            inner = aligned(i * ROWS, ROWS)
            rows = aligned(part * HALF + i * ROWS, ROWS)
            total = None
            for k in range(3):
                values = x_ref[k, rows, :].astype(jnp.float32)
                mean = jnp.sum(values, axis=1, keepdims=True) * (1.0 / ATOMS)
                centred = (values - mean).astype(jnp.bfloat16)
                c_ref[k, rows, :] = centred
                ref[k, inner, :] = centred
                back = centred.astype(jnp.float32)
                square = back * back
                total = square if total is None else total + square
            norms = 0.5 * jnp.sum(total, axis=1, keepdims=True)
            n_ref[rows, :] = jnp.broadcast_to(norms, (ROWS, 128))


def centre(coords):
    return pl.pallas_call(
        centre_kernel,
        in_specs=[VMEM],
        out_specs=[VMEM] * 4,
        out_shape=[
            jax.ShapeDtypeStruct((3, FR, ATOMS), jnp.bfloat16),
            jax.ShapeDtypeStruct((3, HALF, ATOMS), jnp.bfloat16),
            jax.ShapeDtypeStruct((3, HALF, ATOMS), jnp.bfloat16),
            jax.ShapeDtypeStruct((FR, 128), jnp.float32),
        ],
        compiler_params=pltpu.CompilerParams(vmem_limit_bytes=16 << 20),
        name="centre",
    )(coords)


def row_norms(b_ref, rn_ref):
    @pl.loop(0, b_ref.shape[1] // 128)
    def _(i):
        frames = aligned(i * 128, 128)
        total = None
        for k in range(3):
            values = b_ref[k, frames, :].astype(jnp.float32)
            total = values * values if total is None else total + values * values
        norms = 0.5 * jnp.sum(total, axis=1, keepdims=True)
        square = jnp.broadcast_to(norms, (128, 128)).T
        rn_ref[:, frames] = square[0:8, :]


def invariants(entry):
    (a, b, c), (d, f, g), (h, i, j) = entry
    first = a * a + b * b + c * c
    others = (d * d + f * f + g * g) + (h * h + i * i + j * j)
    p = f * j - g * i
    q = g * h - d * j
    r = d * i - f * h
    det = a * p + b * q + c * r
    one = a * d + b * f + c * g
    two = a * h + b * i + c * j
    minors = (first * others - one * one - two * two) + (p * p + q * q + r * r)
    return first + others, det + det, minors


def deviations(entry, left, right):
    n, f, m = invariants(entry)
    start = left + right
    top = start
    for _ in range(NEWTON):
        h = top * top - n
        top = ((h * 0.75 + n) * h + m) * pltpu.reciprocal(top * h - f, approx=True)
    return (start - top) * (2.0 / ATOMS)


def covariance_pieces(a_ref, b_ref, row, col, cov_ref):
    left = a_ref[:, aligned(row, ROWS), :].reshape(3 * ROWS, ATOMS)
    for k in range(3):
        right = b_ref[k, aligned(col, COLS), :]
        block = lax.dot_general(
            left, right, (((1,), (1,)), ((), ())), preferred_element_type=jnp.float32
        )
        cov_ref[:, k] = block.reshape(3, ROWS, COLS)
        yield


def value_pieces(cov_ref, ln_ref, rn_ref, row, col, emit):
    for r in range(0, ROWS, STEP):
        entry = [[cov_ref[k, l, r : r + STEP, :] for l in range(3)] for k in range(3)]
        left = ln_ref[aligned(row + r, STEP), :]
        left = jnp.concatenate([left] * (COLS // 128), axis=1)
        right = rn_ref[:, aligned(col, COLS)]
        right = jnp.concatenate([right] * (STEP // 8), axis=0)
        emit(r, deviations(entry, left, right))
        yield


def run_steps(total, place, a_ref, b_ref, ln_ref, rn_ref, cov0, cov1, old0, old1, keep, turn):
    for _ in covariance_pieces(a_ref, b_ref, *place(0), cov0):
        pass

    def step(s, cov, cov_next, old, old_last):
        row, col = place(jnp.minimum(s + 1, total - 1))
        products = covariance_pieces(a_ref, b_ref, row, col, cov_next)
        row, col = place(s)
        values = value_pieces(cov, ln_ref, rn_ref, row, col, functools.partial(keep, s, old))
        for count, _ in enumerate(values):
            if count in (0, 2, 4):
                next(products)
        turn(jnp.maximum(s - 1, 0), old_last)

    @pl.loop(0, total)
    def _(s):
        @pl.when((s & 1) == 0)
        def _():
            step(s, cov0, cov1, old0, old1)

        @pl.when((s & 1) == 1)
        def _():
            step(s, cov1, cov0, old1, old0)

    turn(total - 1, old1 if total % 2 == 0 else old0)


def encode(values):
    square = values * values
    return (square * square).astype(jnp.bfloat16)


def step_scratch(kind):
    return [
        pltpu.VMEM((3, 3, ROWS, COLS), jnp.float32),
        pltpu.VMEM((3, 3, ROWS, COLS), jnp.float32),
        pltpu.VMEM((ROWS, COLS), kind),
        pltpu.VMEM((ROWS, COLS), kind),
    ]


def diagonal_steps(first, last, a_ref, ln_ref, tile, mirror, rn, scratch):
    row_norms(a_ref, rn)
    per = COLS // ROWS
    starts = [per * c * (c + 1) // 2 for c in range(FR // COLS + 1)]

    def place(s):
        s = s + starts[first]
        col = sum(jnp.where(s >= start, 1, 0) for start in starts[1:last])
        row = s - per * (col * (col + 1) // 2)
        return row * ROWS, col * COLS

    def keep(s, old, r, values):
        row, col = place(s)
        tile[aligned(row + r, STEP), aligned(col, COLS)] = values
        old[r : r + STEP, :] = values

    def turn(s, old):
        row, col = place(s)
        mirror[aligned(col, COLS), aligned(row, ROWS)] = old[...].T

    run_steps(starts[last] - starts[first], place, a_ref, a_ref, ln_ref, rn, *scratch, keep, turn)


def diagonal_kernel(last, a_ref, ln_ref, tile, mirror, rn, *scratch):
    diagonal_steps(0, last, a_ref, ln_ref, tile, mirror, rn, scratch)


def diagonal(centred, norms, last):
    return pl.pallas_call(
        functools.partial(diagonal_kernel, last),
        in_specs=[VMEM, VMEM],
        out_specs=[VMEM, VMEM],
        out_shape=[jax.ShapeDtypeStruct((last * COLS, last * COLS), jnp.float32)] * 2,
        scratch_shapes=[pltpu.VMEM((8, FR), jnp.float32), *step_scratch(jnp.float32)],
        compiler_params=PARAMS,
        cost_estimate=COST,
        name="diagonal",
    )(centred, norms)


def far_kernel(a_ref, b_ref, ln_ref, tile, y_ref, rn, *scratch):
    row_norms(b_ref, rn)
    per = FR // ROWS

    def place(s):
        return (s & (per - 1)) * ROWS, (s // per) * COLS

    def keep(s, old, r, values):
        row, col = place(s)
        tile[aligned(row + r, STEP), aligned(col, COLS)] = values
        old[r : r + STEP, :] = encode(values)

    def turn(s, old):
        row, col = place(s)
        y_ref[aligned(col, COLS), aligned(row, ROWS)] = old[...].T

    run_steps(
        per * (HALF // COLS), place, a_ref, b_ref, ln_ref, rn, *scratch, keep, turn
    )


def far_part(centred, other, norms):
    return pl.pallas_call(
        far_kernel,
        in_specs=[VMEM, VMEM, VMEM],
        out_specs=[VMEM, VMEM],
        out_shape=[
            jax.ShapeDtypeStruct((FR, HALF), jnp.float32),
            jax.ShapeDtypeStruct((HALF, FR), jnp.bfloat16),
        ],
        scratch_shapes=[pltpu.VMEM((8, HALF), jnp.float32), *step_scratch(jnp.bfloat16)],
        compiler_params=PARAMS,
        cost_estimate=COST,
        name="far",
    )(centred, other, norms)


def other_half(half, flip):
    return half + flip - 2 * half * flip


def mate_place():
    parity = lax.rem(lax.axis_index("frames"), 2)
    return 3 - 2 * parity, parity


def near_place():
    parity = lax.rem(lax.axis_index("frames"), 2)
    return 1 + 2 * parity, 1 - parity


def quarters_kernel(where, a_ref, ln_ref, *refs):
    *others, tile, y_ref, b_ref, rn, cov0, cov1, old0, old1, sem = refs
    _, flip = where()
    size = FR // len(others)
    loads = [
        pltpu.make_async_copy(ref, b_ref.at[:, pl.ds(i * size, size)], sem.at[i])
        for i, ref in enumerate(others)
    ]
    for load in loads:
        load.start()
    for load in loads:
        load.wait()
    row_norms(b_ref, rn)
    per_row, per_col = HALF // ROWS, HALF // COLS
    per = per_row * per_col

    def local(s):
        inner = s & (per - 1)
        return s // per, (inner & (per_row - 1)) * ROWS, (inner // per_row) * COLS

    def place(s):
        half, row, col = local(s)
        return half * HALF + row, other_half(half, flip) * HALF + col

    def keep(s, old, r, values):
        half, row, col = local(s)
        tile[half, aligned(row + r, STEP), aligned(col, COLS)] = values
        old[r : r + STEP, :] = encode(values)

    def turn(s, old):
        half, row, col = local(s)
        y_ref[half, aligned(col, COLS), aligned(row, ROWS)] = old[...].T

    run_steps(
        2 * per, place, a_ref, b_ref, ln_ref, rn, cov0, cov1, old0, old1, keep, turn
    )


def quarters(centred, others, norms, where, name):
    return pl.pallas_call(
        functools.partial(quarters_kernel, where),
        in_specs=[VMEM, VMEM] + [ANY] * len(others),
        out_specs=[VMEM, VMEM],
        out_shape=[
            jax.ShapeDtypeStruct((2, HALF, HALF), jnp.float32),
            jax.ShapeDtypeStruct((2, HALF, HALF), jnp.bfloat16),
        ],
        scratch_shapes=[
            pltpu.VMEM((3, FR, ATOMS), jnp.bfloat16),
            pltpu.VMEM((8, FR), jnp.float32),
            *step_scratch(jnp.bfloat16),
            pltpu.SemaphoreType.DMA((len(others),)),
        ],
        compiler_params=PARAMS,
        cost_estimate=COST,
        name=name,
    )(centred, norms, *others)


def decode(values):
    return lax.rsqrt(lax.rsqrt(values.astype(jnp.float32)))


def finish_kernel(
    done, a_ref, ln_ref, diag, turned, far0, far1, near, mate, far0_y, far1_y, near_y, mate_y,
    out_ref, tile, mirror, far_tile, near_tile, mate_tile, rn, *scratch,
):
    *scratch, sem = scratch
    parity = lax.rem(lax.axis_index("frames"), 2)
    copies = []

    def copy(source, slot, rows, cols):
        copies.append(
            pltpu.make_async_copy(source, out_ref.at[slot, rows, cols], sem.at[len(copies)])
        )
        copies[-1].start()

    def half(i):
        return aligned(i * HALF, HALF)

    both = pl.ds(0, FR)
    for i, tiles in enumerate((far0, far1)):
        copy(tiles, 4 * (1 - parity), both, half(i))
    for tiles, where in ((near, near_place), (mate, mate_place)):
        slot, flip = where()
        for i in range(2):
            copy(tiles.at[i], slot, half(i), half(other_half(i, flip)))
    for c in range(done):
        rows, cols = pl.ds(0, (c + 1) * COLS), pl.ds(c * COLS, COLS)
        copy(diag.at[rows, cols], 2, rows, cols)
        if c > 0:
            rows = pl.ds(0, c * COLS)
            copy(turned.at[cols, rows], 2, cols, rows)

    for i, ref in enumerate((far0_y, far1_y)):
        far_tile[i] = decode(ref[...])
        copy(far_tile.at[i], 4 * parity, half(i), both)
    for ref, tiles, where in ((near_y, near_tile, near_place), (mate_y, mate_tile, mate_place)):
        slot, flip = where()
        for i in range(2):
            tiles[i] = decode(ref[i])
            copy(tiles.at[i], slot, half(other_half(i, 1 - flip)), half(i))

    last = FR // COLS
    diagonal_steps(done, last, a_ref, ln_ref, tile, mirror, rn, scratch)
    start = done * COLS
    left, below, right = pl.ds(0, start), pl.ds(start, FR - start), both
    copy(tile.at[right, below], 2, right, below)
    copy(mirror.at[below, left], 2, below, left)
    for each in copies:
        each.wait()


def finish(centred, norms, tiles, coded, done):
    return pl.pallas_call(
        functools.partial(finish_kernel, done),
        in_specs=[VMEM, VMEM] + [ANY] * 6 + [VMEM] * 4,
        out_specs=ANY,
        out_shape=jax.ShapeDtypeStruct((5, FR, FR), jnp.float32),
        scratch_shapes=[
            pltpu.VMEM((FR, FR), jnp.float32),
            pltpu.VMEM((FR, FR), jnp.float32),
            pltpu.VMEM((2, HALF, FR), jnp.float32),
            pltpu.VMEM((2, HALF, HALF), jnp.float32),
            pltpu.VMEM((2, HALF, HALF), jnp.float32),
            pltpu.VMEM((8, FR), jnp.float32),
            *step_scratch(jnp.float32),
            pltpu.SemaphoreType.DMA((32,)),
        ],
        compiler_params=pltpu.CompilerParams(vmem_limit_bytes=26 << 20),
        cost_estimate=COST,
        name="finish",
    )(centred, norms, *tiles, *coded)


def on_device(coords):
    count = lax.axis_size("frames")
    reach = [2 if s % 2 == 0 else -2 for s in range(count)]
    fetch_far = [((s + reach[s]) % count, s) for s in range(count)]
    send_far = [(s, (s + reach[s]) % count) for s in range(count)]
    send_near = [(s, (s - 1 if s % 2 == 0 else s + 1) % count) for s in range(count)]
    swap = [(s, s ^ 1) for s in range(count)]
    move = functools.partial(lax.ppermute, axis_name="frames")

    centred, low, high, norms = centre(coords)
    far_low = move(low, perm=fetch_far)
    far_high = move(high, perm=fetch_far)
    mate = move(centred, perm=swap)
    done = FR // COLS - 1
    diag, turned = diagonal(centred, norms, done)
    far_low, diag = lax.optimization_barrier((far_low, diag))
    near_low = move(far_low, perm=swap)
    far0, far0_y = far_part(centred, far_low, norms)
    far_high, far0, far0_y = lax.optimization_barrier((far_high, far0, far0_y))
    near_high = move(far_high, perm=swap)
    far0_y = move(far0_y, perm=send_far)
    far1, far1_y = far_part(centred, far_high, norms)
    centred, far1_y = lax.optimization_barrier((centred, far1_y))
    far1_y = move(far1_y, perm=send_far)
    near, near_y = quarters(centred, (near_low, near_high), norms, near_place, "near")
    centred, near_y = lax.optimization_barrier((centred, near_y))
    near_y = move(near_y, perm=send_near)
    mate, mate_y = quarters(centred, (mate,), norms, mate_place, "mate")
    mate_y = move(mate_y, perm=swap)
    tiles = (diag, turned, far0, far1, near, mate)
    out = finish(centred, norms, tiles, (far0_y, far1_y, near_y, mate_y), done)
    return jnp.transpose(out, (1, 0, 2))


def solution(mesh):
    return jax.shard_map(
        on_device,
        mesh=mesh,
        in_specs=(P(None, "frames", None),),
        out_specs=P("frames", None, None),
        check_vma=False,
    )
```

```python
import functools

import jax
import jax.numpy as jnp
from jax import lax
from jax.experimental import pallas as pl
from jax.experimental.pallas import tpu as pltpu
from jax.sharding import PartitionSpec as P

NEWTON = 8
FR = 1024
ATOMS = 256
ROWS = 128
COLS = 256
STEP = 16
HALF = FR // 2
VMEM = pl.BlockSpec(memory_space=pltpu.VMEM)
ANY = pl.BlockSpec(memory_space=pl.ANY)
VMEM_LIMIT = 14 << 20


def aligned(index, size):
    return pl.ds(pl.multiple_of(index, size), size)


def norm_rows(total):
    norms = jnp.broadcast_to(0.5 * jnp.sum(total, axis=1, keepdims=True), (128, 128))
    return norms, norms.T[0:8, :]


def centre(x_ref, all_ref, ln_ref, rn_ref, first, count):
    @pl.loop(first // 128, (first + count) // 128)
    def _(i):
        rows = aligned(i * 128, 128)
        total = None
        for k in range(3):
            values = x_ref[k, rows, :].astype(jnp.float32)
            mean = jnp.sum(values, axis=1, keepdims=True) * (1.0 / ATOMS)
            centred = (values - mean).astype(jnp.bfloat16)
            all_ref[k, rows, :] = centred
            back = centred.astype(jnp.float32)
            total = back * back if total is None else total + back * back
        ln_ref[rows, :], rn_ref[:, rows] = norm_rows(total)


def row_norms(all_ref, rn_ref, first, count):
    @pl.loop(0, count // 128)
    def _(i):
        frames = aligned(first + i * 128, 128)
        total = None
        for k in range(3):
            values = all_ref[k, frames, :].astype(jnp.float32)
            total = values * values if total is None else total + values * values
        rn_ref[:, frames] = norm_rows(total)[1]


def invariants(entry):
    (a, b, c), (d, f, g), (h, i, j) = entry
    first = a * a + b * b + c * c
    others = (d * d + f * f + g * g) + (h * h + i * i + j * j)
    p = f * j - g * i
    q = g * h - d * j
    r = d * i - f * h
    det = a * p + b * q + c * r
    one = a * d + b * f + c * g
    two = a * h + b * i + c * j
    minors = (first * others - one * one - two * two) + (p * p + q * q + r * r)
    return first + others, det + det, minors


def deviations(entry, left, right):
    n, f, m = invariants(entry)
    start = left + right
    top = start
    for _ in range(NEWTON):
        h = top * top - n
        top = ((h * 0.75 + n) * h + m) * pltpu.reciprocal(top * h - f, approx=True)
    return (start - top) * (2.0 / ATOMS)


def covariance_pieces(all_ref, row, col, cov_ref):
    left = all_ref[:, aligned(row, ROWS), :].reshape(3 * ROWS, ATOMS)
    for k in range(3):
        right = all_ref[k, aligned(col, COLS), :]
        block = lax.dot_general(
            left, right, (((1,), (1,)), ((), ())), preferred_element_type=jnp.float32
        )
        cov_ref[:, k] = block.reshape(3, ROWS, COLS)
        yield


def value_pieces(cov_ref, ln_ref, rn_ref, row, col):
    for r in range(0, ROWS, STEP):
        entry = [[cov_ref[k, l, r : r + STEP, :] for l in range(3)] for k in range(3)]
        left = ln_ref[aligned(row + r, STEP), :]
        left = jnp.concatenate([left] * (COLS // 128), axis=1)
        right = rn_ref[:, aligned(col, COLS)]
        right = jnp.concatenate([right] * (STEP // 8), axis=0)
        yield r, deviations(entry, left, right)


def encode(values):
    square = values * values
    return (square * square).astype(jnp.bfloat16)


def other_half(half, flip):
    return half + flip - 2 * half * flip


def mate_place(parity):
    return 3 - 2 * parity, parity


def near_place(parity):
    return 1 + 2 * parity, 1 - parity


OWN, FAR, NEAR, MATE = range(0, 4 * FR, FR)
FAR_AT, NEAR_AT, MATE_AT, LAST_AT, STEPS = 12, 44, 60, 76, 84
CHUNKS = FR // COLS


def step_place(s, parity):
    early = jnp.where(s >= 2, 1, 0) + jnp.where(s >= 6, 1, 0)
    is_last = s >= LAST_AT
    row = jnp.where(is_last, s - LAST_AT, s - early * (early + 1))
    col = jnp.where(is_last, 3 * COLS, early * COLS)

    far = s - FAR_AT
    is_far = s >= FAR_AT
    row = jnp.where(is_far & (s < NEAR_AT), far & 7, row)
    col = jnp.where(is_far & (s < NEAR_AT), FAR + (far >> 3) * COLS, col)

    inner = (s - NEAR_AT) & 15
    is_mate = s >= MATE_AT
    flip = jnp.where(is_mate, parity, 1 - parity)
    half = inner >> 3
    is_quarter = (s >= NEAR_AT) & (s < LAST_AT)
    row = jnp.where(is_quarter, half * (HALF // ROWS) + (inner & 3), row)
    base = jnp.where(is_mate, MATE, NEAR) + ((inner >> 2) & 1) * COLS
    col = jnp.where(is_quarter, base + other_half(half, flip) * HALF, col)
    return row * ROWS, col


def main_kernel(
    count, x_ref, tile, y_ref, got_ref, all_ref, ln_ref, rn_ref, cov0, cov1, old0, old1,
    far_sems, near_sems, mate_sems, far_y_sems, near_y_sems, mate_y_sems,
):
    me = lax.axis_index("frames")
    parity = lax.rem(me, 2)
    way = 1 - 2 * parity
    far = lax.rem(me + 2 * way + count, count)
    far_back = lax.rem(me - 2 * way + count, count)
    near = lax.rem(me - way + count, count)
    mate = me + way

    barrier = pltpu.get_barrier_semaphore()
    for device in (far, far_back, near, mate):
        pl.semaphore_signal(
            barrier, inc=1, device_id=(device,), device_id_type=pl.DeviceIdType.MESH
        )

    def remote(source, target, sems, i, device):
        return pltpu.make_async_remote_copy(
            src_ref=source,
            dst_ref=target,
            send_sem=sems.at[0, i],
            recv_sem=sems.at[1, i],
            device_id=(device,),
            device_id_type=pl.DeviceIdType.MESH,
        )

    def frames(block, i):
        return all_ref.at[:, aligned(block + i * COLS, COLS)]

    def far_copy(i):
        return remote(frames(OWN, i), frames(FAR, i), far_sems, i, far_back)

    def near_copy(i):
        return remote(frames(FAR, i), frames(NEAR, i), near_sems, i, mate)

    def mate_copy(i):
        return remote(frames(OWN, i), frames(MATE, i), mate_sems, i, mate)

    def far_y_copy(i):
        rows = aligned(i * COLS, COLS)
        source = y_ref.at[aligned(FAR + i * COLS, COLS)]
        return remote(source, got_ref.at[rows], far_y_sems, i, far)

    def quarter_y_copy(block, flip, i, sems, device):
        half = i >> 1
        row = block + other_half(half, flip) * HALF + (i & 1) * COLS
        cols = aligned(half * HALF, HALF)
        source = y_ref.at[aligned(row, COLS), cols]
        return remote(source, got_ref.at[aligned(row - FAR, COLS), cols], sems, i, device)

    def near_y_copy(i):
        return quarter_y_copy(NEAR, 1 - parity, i, near_y_sems, near)

    def mate_y_copy(i):
        return quarter_y_copy(MATE, parity, i, mate_y_sems, mate)

    for i in range(CHUNKS):
        centre(x_ref, all_ref, ln_ref, rn_ref, i * COLS, COLS)
        if i == 0:
            pl.semaphore_wait(barrier, 4)
        far_copy(i).start()
        mate_copy(i).start()

    def take(group):
        @pl.when((group >= 2) & (group <= 8) & ((group & 1) == 0))
        def _():
            i = (group - 2) >> 1
            far_copy(i).wait_recv()
            near_copy(i).start()
            row_norms(all_ref, rn_ref, FAR + i * COLS, COLS)

        @pl.when(group == NEAR_AT // 4 - 1)
        def _():
            for i in range(CHUNKS):
                near_copy(i).wait_recv()
            row_norms(all_ref, rn_ref, NEAR, FR)

        @pl.when(group == MATE_AT // 4 - 1)
        def _():
            for i in range(CHUNKS):
                mate_copy(i).wait_recv()
            row_norms(all_ref, rn_ref, MATE, FR)

    def give(group):
        @pl.when((group >= 5) & (group <= 11) & ((group & 1) == 1))
        def _():
            far_y_copy((group - 5) >> 1).start()

        @pl.when((group > NEAR_AT // 4) & (group <= MATE_AT // 4))
        def _():
            near_y_copy(group - NEAR_AT // 4 - 1).start()

        @pl.when((group > MATE_AT // 4) & (group <= LAST_AT // 4))
        def _():
            mate_y_copy(group - MATE_AT // 4 - 1).start()

    def turn(row, col, old):
        y_ref[aligned(col, COLS), aligned(row, ROWS)] = old[...].T

    def step(places, cov, cov_next, old, old_last):
        (row_last, col_last), (row, col), (row_next, col_next) = places
        products = covariance_pieces(all_ref, row_next, col_next, cov_next)
        for piece, (r, values) in enumerate(value_pieces(cov, ln_ref, rn_ref, row, col)):
            tile[aligned(row + r, STEP), aligned(col, COLS)] = values
            old[r : r + STEP, :] = encode(values)
            if piece in (0, 2, 4):
                next(products)
        turn(row_last, col_last, old_last)

    first = step_place(jnp.int32(0), parity)
    for _ in covariance_pieces(all_ref, *first, cov0):
        pass
    old1[...] = jnp.zeros_like(old1)

    def body(s, places):
        @pl.when((s & 3) == 0)
        def _():
            take(s >> 2)

        @pl.when((s & 3) == 1)
        def _():
            give(s >> 2)

        @pl.when((s & 1) == 0)
        def _():
            step(places, cov0, cov1, old0, old1)

        @pl.when((s & 1) == 1)
        def _():
            step(places, cov1, cov0, old1, old0)

        return places[1], places[2], step_place(jnp.minimum(s + 2, STEPS - 1), parity)

    start = (first, first, step_place(jnp.int32(1), parity))
    places = lax.fori_loop(0, STEPS, body, start)
    turn(*places[0], old1)

    for i in range(CHUNKS):
        far_copy(i).wait_send()
        mate_copy(i).wait_send()
        near_copy(i).wait_send()
        far_y_copy(i).wait()
        near_y_copy(i).wait()
        mate_y_copy(i).wait()


def main(coords, count):
    pair = pltpu.SemaphoreType.DMA((2, CHUNKS))
    return pl.pallas_call(
        functools.partial(main_kernel, count),
        in_specs=[VMEM],
        out_specs=[VMEM] * 3,
        out_shape=[
            jax.ShapeDtypeStruct((FR, 4 * FR), jnp.float32),
            jax.ShapeDtypeStruct((4 * FR, FR), jnp.bfloat16),
            jax.ShapeDtypeStruct((3 * FR, FR), jnp.bfloat16),
        ],
        scratch_shapes=[
            pltpu.VMEM((3, 4 * FR, ATOMS), jnp.bfloat16),
            pltpu.VMEM((FR, 128), jnp.float32),
            pltpu.VMEM((8, 4 * FR), jnp.float32),
            pltpu.VMEM((3, 3, ROWS, COLS), jnp.float32),
            pltpu.VMEM((3, 3, ROWS, COLS), jnp.float32),
            pltpu.VMEM((ROWS, COLS), jnp.bfloat16),
            pltpu.VMEM((ROWS, COLS), jnp.bfloat16),
            *[pair] * 6,
        ],
        compiler_params=pltpu.CompilerParams(
            collective_id=0, has_side_effects=True, vmem_limit_bytes=VMEM_LIMIT
        ),
        cost_estimate=pl.CostEstimate(
            flops=45 * FR * FR * ATOMS, bytes_accessed=32 << 20, transcendentals=0
        ),
        name="deviations",
    )(coords)


def decode(values):
    return lax.rsqrt(lax.rsqrt(values.astype(jnp.float32)))


def finish_kernel(tile, y_ref, got_ref, out_ref, far_tile, near_tile, mate_tile, low_tile, sem):
    parity = lax.rem(lax.axis_index("frames"), 2)
    copies = []

    def copy(source, slot, rows, cols):
        copies.append(
            pltpu.make_async_copy(source, out_ref.at[slot, rows, cols], sem.at[len(copies)])
        )
        copies[-1].start()

    def half(i, base=0):
        return pl.ds(pl.multiple_of(base + i * HALF, HALF), HALF)

    both = pl.ds(0, FR)
    quarters = ((NEAR, near_place(parity), near_tile), (MATE, mate_place(parity), mate_tile))
    copy(tile.at[:, pl.ds(FAR, FR)], 4 * (1 - parity), both, both)
    for block, (slot, flip), _ in quarters:
        for i in range(2):
            other = other_half(i, flip)
            copy(tile.at[half(i), half(other, block)], slot, half(i), half(other))
    for c in range(CHUNKS):
        rows, cols = pl.ds(0, (c + 1) * COLS), pl.ds(c * COLS, COLS)
        copy(tile.at[rows, cols], 2, rows, cols)

    for i in range(CHUNKS):
        rows = pl.ds(i * COLS, COLS)
        far_tile[rows, :] = decode(got_ref[rows, :])
        copy(far_tile.at[rows], 4 * parity, rows, both)
    for block, (slot, flip), tiles in quarters:
        for i in range(2):
            own = other_half(i, 1 - flip)
            tiles[i] = decode(got_ref[half(own, block - FAR), half(i)])
            copy(tiles.at[i], slot, half(own), half(i))
    for c in range(1, CHUNKS):
        rows, cols = pl.ds(c * COLS, COLS), pl.ds(0, c * COLS)
        low_tile[rows, cols] = decode(y_ref[rows, cols])
        copy(low_tile.at[rows, cols], 2, rows, cols)
    for each in copies:
        each.wait()


def finish(tile, y, got):
    return pl.pallas_call(
        finish_kernel,
        in_specs=[ANY, VMEM, VMEM],
        out_specs=ANY,
        out_shape=jax.ShapeDtypeStruct((5, FR, FR), jnp.float32),
        scratch_shapes=[
            pltpu.VMEM((FR, FR), jnp.float32),
            pltpu.VMEM((2, HALF, HALF), jnp.float32),
            pltpu.VMEM((2, HALF, HALF), jnp.float32),
            pltpu.VMEM((FR, FR), jnp.float32),
            pltpu.SemaphoreType.DMA((32,)),
        ],
        compiler_params=pltpu.CompilerParams(vmem_limit_bytes=VMEM_LIMIT),
        name="finish",
    )(tile, y, got)


def on_device(coords):
    out = finish(*main(coords, lax.axis_size("frames")))
    return jnp.transpose(out, (1, 0, 2))


def solution(mesh):
    return jax.shard_map(
        on_device,
        mesh=mesh,
        in_specs=(P(None, "frames", None),),
        out_specs=P("frames", None, None),
        check_vma=False,
    )
```

```python
import functools

import jax
import jax.numpy as jnp
from jax import lax
from jax.experimental import pallas as pl
from jax.experimental.pallas import tpu as pltpu
from jax.sharding import PartitionSpec as P

NEWTON = 8
FR = 1024
ATOMS = 256
ROWS = 256
COLS = 256
STEP = 16
HALF = FR // 2
VMEM = pl.BlockSpec(memory_space=pltpu.VMEM)
ANY = pl.BlockSpec(memory_space=pl.ANY)
MAIN_LIMIT = 15 << 20
FINISH_LIMIT = 13 << 20


def aligned(index, size):
    return pl.ds(pl.multiple_of(index, size), size)


def centre(x_ref, all_ref, ln_ref, rn_ref):
    weights = jnp.full((ATOMS, 128), 1.0 / ATOMS, jnp.bfloat16)

    @pl.loop(0, FR // 128)
    def _(i):
        rows = aligned(i * 128, 128)
        total = None
        for k in range(3):
            values = x_ref[k, rows, :]
            mean = jnp.dot(values, weights, preferred_element_type=jnp.float32)
            mean = jnp.concatenate([mean] * (ATOMS // 128), axis=1)
            centred = (values.astype(jnp.float32) - mean).astype(jnp.bfloat16)
            all_ref[k, rows, :] = centred
            back = centred.astype(jnp.float32)
            total = back * back if total is None else total + back * back
        norms = jnp.broadcast_to(0.5 * jnp.sum(total, axis=1, keepdims=True), (128, 128))
        ln_ref[rows, :] = norms
        rn_ref[:, rows] = norms.T[0:8, :]


def invariants(entry):
    (a, b, c), (d, f, g), (h, i, j) = entry
    first = a * a + b * b + c * c
    others = (d * d + f * f + g * g) + (h * h + i * i + j * j)
    p = f * j - g * i
    q = g * h - d * j
    r = d * i - f * h
    det = a * p + b * q + c * r
    one = a * d + b * f + c * g
    two = a * h + b * i + c * j
    minors = (first * others - one * one - two * two) + (p * p + q * q + r * r)
    return first + others, det + det, minors


def deviations(entry, left, right):
    n, f, m = invariants(entry)
    start = left + right
    top = start
    for _ in range(NEWTON):
        h = top * top - n
        top = ((h * 0.75 + n) * h + m) * pltpu.reciprocal(top * h - f, approx=True)
    return (start - top) * (2.0 / ATOMS)


def covariance_pieces(all_ref, row, col, cov_ref):
    left = all_ref[:, aligned(row, ROWS), :].reshape(3 * ROWS, ATOMS)
    for k in range(3):
        right = all_ref[k, aligned(col, COLS), :]
        block = lax.dot_general(
            left, right, (((1,), (1,)), ((), ())), preferred_element_type=jnp.float32
        )
        cov_ref[:, k] = block.reshape(3, ROWS, COLS)
        yield


def value_pieces(cov_ref, ln_ref, rn_ref, row, col):
    for r in range(0, ROWS, STEP):
        entry = [[cov_ref[k, l, r : r + STEP, :] for l in range(3)] for k in range(3)]
        left = ln_ref[aligned(row + r, STEP), :]
        left = jnp.concatenate([left] * (COLS // 128), axis=1)
        right = rn_ref[:, aligned(col, COLS)]
        right = jnp.concatenate([right] * (STEP // 8), axis=0)
        yield r, deviations(entry, left, right)


def encode(values):
    square = values * values
    return (square * square).astype(jnp.bfloat16)


def other_half(half, flip):
    return half + flip - 2 * half * flip


def mate_place(parity):
    return 3 - 2 * parity, parity


def near_place(parity):
    return 1 + 2 * parity, 1 - parity


OWN, FAR, NEAR, MATE = range(0, 4 * FR, FR)
FAR_AT, NEAR_AT, MATE_AT, GROUPS = 5, 13, 17, 21
SPLIT = 2
CHUNKS = FR // COLS


def group_place(g, parity):
    row = jnp.where(g == SPLIT, 2, jnp.where(g == FAR_AT - 1, 2, 0))
    col = jnp.where(g == 0, 1, jnp.where(g <= SPLIT, 2, 3)) * COLS

    far = g - FAR_AT
    is_far = g >= FAR_AT
    row = jnp.where(is_far, (far & 1) * 2, row)
    col = jnp.where(is_far, FAR + (far >> 1) * COLS, col)

    inner = (g - NEAR_AT) & 3
    is_quarter, is_mate = g >= NEAR_AT, g >= MATE_AT
    flip = jnp.where(is_mate, parity, 1 - parity)
    half = inner >> 1
    row = jnp.where(is_quarter, half * 2, row)
    base = jnp.where(is_mate, MATE, NEAR) + (inner & 1) * COLS
    col = jnp.where(is_quarter, base + other_half(half, flip) * HALF, col)
    return row * ROWS, col


def second_place(g, first):
    row, col = first
    return jnp.where(g == SPLIT, 0, row + ROWS), jnp.where(g == SPLIT, 0, col)


def main_kernel(
    count, x_ref, tile, y_ref, got_ref, all_ref, ln_ref, rn_ref, cov0, cov1, old0, old1,
    far_sems, near_sems, mate_sems, far_y_sems, near_y_sems, mate_y_sems,
    far_n_sems, near_n_sems, mate_n_sems,
):
    me = lax.axis_index("frames")
    parity = lax.rem(me, 2)
    way = 1 - 2 * parity
    far = lax.rem(me + 2 * way + count, count)
    far_back = lax.rem(me - 2 * way + count, count)
    near = lax.rem(me - way + count, count)
    mate = me + way

    barrier = pltpu.get_barrier_semaphore()
    for device in (far, far_back, near, mate):
        pl.semaphore_signal(
            barrier, inc=1, device_id=(device,), device_id_type=pl.DeviceIdType.MESH
        )

    def remote(source, target, sems, i, device):
        return pltpu.make_async_remote_copy(
            src_ref=source,
            dst_ref=target,
            send_sem=sems.at[0, i],
            recv_sem=sems.at[1, i],
            device_id=(device,),
            device_id_type=pl.DeviceIdType.MESH,
        )

    def frames(block, i):
        return all_ref.at[:, aligned(block + i * COLS, COLS)]

    def norms(block, i):
        return rn_ref.at[:, aligned(block + i * COLS, COLS)]

    def far_copies(i):
        return (
            remote(frames(OWN, i), frames(FAR, i), far_sems, i, far_back),
            remote(norms(OWN, i), norms(FAR, i), far_n_sems, i, far_back),
        )

    def near_copies(i):
        return (
            remote(frames(FAR, i), frames(NEAR, i), near_sems, i, mate),
            remote(norms(FAR, i), norms(NEAR, i), near_n_sems, i, mate),
        )

    def mate_copies(i):
        return (
            remote(frames(OWN, i), frames(MATE, i), mate_sems, i, mate),
            remote(norms(OWN, i), norms(MATE, i), mate_n_sems, i, mate),
        )

    def far_y_copy(i):
        rows = aligned(i * COLS, COLS)
        source = y_ref.at[aligned(FAR + i * COLS, COLS)]
        return remote(source, got_ref.at[rows], far_y_sems, i, far)

    def quarter_y_copy(block, flip, i, sems, device):
        half = i >> 1
        row = block + other_half(half, flip) * HALF + (i & 1) * COLS
        cols = aligned(half * HALF, HALF)
        source = y_ref.at[aligned(row, COLS), cols]
        return remote(source, got_ref.at[aligned(row - FAR, COLS), cols], sems, i, device)

    def near_y_copy(i):
        return quarter_y_copy(NEAR, 1 - parity, i, near_y_sems, near)

    def mate_y_copy(i):
        return quarter_y_copy(MATE, parity, i, mate_y_sems, mate)

    centre(x_ref, all_ref, ln_ref, rn_ref)

    def begin(group):
        @pl.when(group == 1)
        def _():
            pl.semaphore_wait(barrier, 4)
            for i in range(CHUNKS):
                for copy in (*far_copies(i), *mate_copies(i)):
                    copy.start()

    def take(group):
        @pl.when((group >= FAR_AT - 1) & (group < NEAR_AT - 1) & ((group & 1) == 0))
        def _():
            i = (group - FAR_AT + 1) >> 1
            for copy in far_copies(i):
                copy.wait_recv()
            for copy in near_copies(i):
                copy.start()

        @pl.when(group == NEAR_AT - 1)
        def _():
            for i in range(CHUNKS):
                for copy in near_copies(i):
                    copy.wait_recv()

        @pl.when(group == MATE_AT - 1)
        def _():
            for i in range(CHUNKS):
                for copy in mate_copies(i):
                    copy.wait_recv()

    def give(group):
        @pl.when((group > FAR_AT + 1) & (group <= NEAR_AT) & ((group & 1) == 1))
        def _():
            far_y_copy((group - FAR_AT - 2) >> 1).start()

        @pl.when((group > NEAR_AT) & (group <= MATE_AT))
        def _():
            near_y_copy(group - NEAR_AT - 1).start()

        @pl.when(group > MATE_AT)
        def _():
            mate_y_copy(group - MATE_AT - 1).start()

    def turn(row, col, old):
        y_ref[aligned(col, COLS), aligned(row, ROWS)] = old[...].T

    def step(last, now, following, cov, cov_next, old, old_last):
        row, col = now
        products = covariance_pieces(all_ref, *following, cov_next)
        for piece, (r, values) in enumerate(value_pieces(cov, ln_ref, rn_ref, row, col)):
            tile[aligned(row + r, STEP), aligned(col, COLS)] = values
            old[r : r + STEP, :] = encode(values)
            if piece in (2, 8, 13):
                next(products)
        turn(*last, old_last)

    first = group_place(jnp.int32(0), parity)
    for _ in covariance_pieces(all_ref, *first, cov0):
        pass
    old1[...] = jnp.zeros_like(old1)

    def body(group, places):
        last, now = places
        second = second_place(group, now)
        following = group_place(jnp.minimum(group + 1, GROUPS - 1), parity)
        begin(group)
        step(last, now, second, cov0, cov1, old0, old1)
        take(group)
        give(group)
        step(now, second, following, cov1, cov0, old1, old0)
        return second, following

    last, _ = lax.fori_loop(0, GROUPS, body, (first, first))
    turn(*last, old1)
    mate_y_copy(CHUNKS - 1).start()

    for i in range(CHUNKS):
        for copy in (*far_copies(i), *mate_copies(i), *near_copies(i)):
            copy.wait_send()
        far_y_copy(i).wait()
        near_y_copy(i).wait()
        mate_y_copy(i).wait()


def main(coords, count):
    pair = pltpu.SemaphoreType.DMA((2, CHUNKS))
    return pl.pallas_call(
        functools.partial(main_kernel, count),
        in_specs=[VMEM],
        out_specs=[VMEM] * 3,
        out_shape=[
            jax.ShapeDtypeStruct((FR, 4 * FR), jnp.float32),
            jax.ShapeDtypeStruct((4 * FR, FR), jnp.bfloat16),
            jax.ShapeDtypeStruct((3 * FR, FR), jnp.bfloat16),
        ],
        scratch_shapes=[
            pltpu.VMEM((3, 4 * FR, ATOMS), jnp.bfloat16),
            pltpu.VMEM((FR, 128), jnp.float32),
            pltpu.VMEM((8, 4 * FR), jnp.float32),
            pltpu.VMEM((3, 3, ROWS, COLS), jnp.float32),
            pltpu.VMEM((3, 3, ROWS, COLS), jnp.float32),
            pltpu.VMEM((ROWS, COLS), jnp.bfloat16),
            pltpu.VMEM((ROWS, COLS), jnp.bfloat16),
            *[pair] * 9,
        ],
        compiler_params=pltpu.CompilerParams(
            collective_id=0, has_side_effects=True, vmem_limit_bytes=MAIN_LIMIT
        ),
        cost_estimate=pl.CostEstimate(
            flops=45 * FR * FR * ATOMS, bytes_accessed=32 << 20, transcendentals=0
        ),
        name="deviations",
    )(coords)


def decode(values):
    return lax.rsqrt(lax.rsqrt(values.astype(jnp.float32)))


def finish_kernel(tile, y_ref, got_ref, out_ref, far_tile, near_tile, mate_tile, low_tile, sem):
    parity = lax.rem(lax.axis_index("frames"), 2)
    copies = []

    def copy(source, slot, rows, cols):
        copies.append(
            pltpu.make_async_copy(source, out_ref.at[slot, rows, cols], sem.at[len(copies)])
        )
        copies[-1].start()

    def half(i, base=0):
        return pl.ds(pl.multiple_of(base + i * HALF, HALF), HALF)

    both = pl.ds(0, FR)
    quarters = ((NEAR, near_place(parity), near_tile), (MATE, mate_place(parity), mate_tile))
    copy(tile.at[:, pl.ds(FAR, FR)], 4 * (1 - parity), both, both)
    for block, (slot, flip), _ in quarters:
        for i in range(2):
            other = other_half(i, flip)
            copy(tile.at[half(i), half(other, block)], slot, half(i), half(other))
    for c in range(CHUNKS):
        rows, cols = pl.ds(0, (c + 1) * COLS), pl.ds(c * COLS, COLS)
        copy(tile.at[rows, cols], 2, rows, cols)

    for i in range(CHUNKS):
        rows = pl.ds(i * COLS, COLS)
        far_tile[rows, :] = decode(got_ref[rows, :])
        copy(far_tile.at[rows], 4 * parity, rows, both)
    for block, (slot, flip), tiles in quarters:
        for i in range(2):
            own = other_half(i, 1 - flip)
            tiles[i] = decode(got_ref[half(own, block - FAR), half(i)])
            copy(tiles.at[i], slot, half(own), half(i))
    for c in range(1, CHUNKS):
        rows, cols = pl.ds(c * COLS, COLS), pl.ds(0, c * COLS)
        low_tile[rows, cols] = decode(y_ref[rows, cols])
        copy(low_tile.at[rows, cols], 2, rows, cols)
    for each in copies:
        each.wait()


def finish(tile, y, got):
    return pl.pallas_call(
        finish_kernel,
        in_specs=[ANY, VMEM, VMEM],
        out_specs=ANY,
        out_shape=jax.ShapeDtypeStruct((5, FR, FR), jnp.float32),
        scratch_shapes=[
            pltpu.VMEM((FR, FR), jnp.float32),
            pltpu.VMEM((2, HALF, HALF), jnp.float32),
            pltpu.VMEM((2, HALF, HALF), jnp.float32),
            pltpu.VMEM((FR, FR), jnp.float32),
            pltpu.SemaphoreType.DMA((32,)),
        ],
        compiler_params=pltpu.CompilerParams(vmem_limit_bytes=FINISH_LIMIT),
        name="finish",
    )(tile, y, got)


def on_device(coords):
    out = finish(*main(coords, lax.axis_size("frames")))
    return jnp.transpose(out, (1, 0, 2))


def solution(mesh):
    return jax.shard_map(
        on_device,
        mesh=mesh,
        in_specs=(P(None, "frames", None),),
        out_specs=P("frames", None, None),
        check_vma=False,
    )
```

```python
import functools

import jax
import jax.numpy as jnp
from jax import lax
from jax.experimental import pallas as pl
from jax.experimental.pallas import tpu as pltpu
from jax.sharding import PartitionSpec as P

NEWTON = 8
FR = 1024
ATOMS = 256
ROWS = 256
COLS = 256
STEP = 16
HALF = FR // 2
VMEM = pl.BlockSpec(memory_space=pltpu.VMEM)
ANY = pl.BlockSpec(memory_space=pl.ANY)
MAIN_LIMIT = 12 << 20
FINISH_LIMIT = 22 << 20


def aligned(index, size):
    if isinstance(index, int):
        return pl.ds(index, size)
    return pl.ds(pl.multiple_of(index, size), size)


def centre(x_ref, all_ref, own_ref, ln_ref, rn_ref):
    weights = jnp.full((ATOMS, 128), 1.0 / ATOMS, jnp.bfloat16)

    @pl.loop(0, FR // 128)
    def _(i):
        rows = aligned(i * 128, 128)
        total = None
        for k in range(3):
            values = x_ref[k, rows, :]
            mean = jnp.dot(values, weights, preferred_element_type=jnp.float32)
            mean = jnp.concatenate([mean] * (ATOMS // 128), axis=1)
            centred = (values.astype(jnp.float32) - mean).astype(jnp.bfloat16)
            all_ref[k, rows, :] = centred
            own_ref[k, rows, :] = centred
            back = centred.astype(jnp.float32)
            total = back * back if total is None else total + back * back
        norms = jnp.broadcast_to(0.5 * jnp.sum(total, axis=1, keepdims=True), (128, 128))
        ln_ref[rows, :] = norms
        rn_ref[:, rows] = norms.T[0:8, :]


def invariants(entry):
    (a, b, c), (d, f, g), (h, i, j) = entry
    first = a * a + b * b + c * c
    others = (d * d + f * f + g * g) + (h * h + i * i + j * j)
    p = f * j - g * i
    q = g * h - d * j
    r = d * i - f * h
    det = a * p + b * q + c * r
    one = a * d + b * f + c * g
    two = a * h + b * i + c * j
    minors = (first * others - one * one - two * two) + (p * p + q * q + r * r)
    return first + others, det + det, minors


def deviations(entry, left, right):
    n, f, m = invariants(entry)
    start = left + right
    top = start
    for _ in range(NEWTON):
        h = top * top - n
        top = ((h * 0.75 + n) * h + m) * pltpu.reciprocal(top * h - f, approx=True)
    return (start - top) * (2.0 / ATOMS)


def covariance_pieces(all_ref, row, col, cov_ref):
    left = all_ref[:, aligned(row, ROWS), :].reshape(3 * ROWS, ATOMS)
    for k in range(3):
        right = all_ref[k, aligned(col, COLS), :]
        block = lax.dot_general(
            left, right, (((1,), (1,)), ((), ())), preferred_element_type=jnp.float32
        )
        cov_ref[:, k] = block.reshape(3, ROWS, COLS)
        yield


def interleave(values, products):
    for piece, value in enumerate(values):
        yield piece, value
        if piece in (2, 8, 13):
            next(products, None)


def value_pieces(cov_ref, ln_ref, rn_ref, row, col):
    for r in range(0, ROWS, STEP):
        entry = [[cov_ref[k, l, r : r + STEP, :] for l in range(3)] for k in range(3)]
        left = ln_ref[aligned(row + r, STEP), :]
        left = jnp.concatenate([left] * (COLS // 128), axis=1)
        right = rn_ref[:, aligned(col, COLS)]
        right = jnp.concatenate([right] * (STEP // 8), axis=0)
        yield r, deviations(entry, left, right)


def encode(values):
    square = values * values
    return (square * square).astype(jnp.bfloat16)


def other_half(half, flip):
    return half + flip - 2 * half * flip


def mate_place(parity):
    return 3 - 2 * parity, parity


def near_place(parity):
    return 1 + 2 * parity, 1 - parity


OWN, FAR, NEAR, MATE = range(0, 4 * FR, FR)
NEAR_OUT, MATE_OUT, WIDTH = 2 * FR, 2 * FR + HALF, 3 * FR
FAR_AT, NEAR_AT, MATE_AT, GROUPS = 3, 11, 15, 19
SPLIT = 2
CHUNKS = FR // COLS
LAST = FR - COLS


def group_place(g, parity):
    row = jnp.where(g == SPLIT, 2, 0)
    col = jnp.where(g == 0, 1, 2) * COLS

    far = g - FAR_AT
    is_far = g >= FAR_AT
    row = jnp.where(is_far, (far & 1) * 2, row)
    col = jnp.where(is_far, FAR + (far >> 1) * COLS, col)

    inner = (g - NEAR_AT) & 3
    is_quarter, is_mate = g >= NEAR_AT, g >= MATE_AT
    flip = jnp.where(is_mate, parity, 1 - parity)
    half = inner >> 1
    row = jnp.where(is_quarter, half * 2, row)
    inside = (inner & 1) * COLS
    out = jnp.where(is_quarter, jnp.where(is_mate, MATE_OUT, NEAR_OUT) + inside, col)
    base = jnp.where(is_mate, MATE, NEAR) + inside
    col = jnp.where(is_quarter, base + other_half(half, flip) * HALF, col)
    return row * ROWS, col, out


def second_place(g, first):
    row, col, out = first
    return tuple(jnp.where(g == SPLIT, 0, each) for each in (row + ROWS, col, out))


def main_kernel(
    count, x_ref, tile, y_ref, got_ref, own_ref, ln_ref, rn_ref,
    all_ref, cov0, cov1, old0, old1,
    far_sems, near_sems, mate_sems, far_y_sems, near_y_sems, mate_y_sems,
    far_n_sems, near_n_sems, mate_n_sems,
):
    me = lax.axis_index("frames")
    parity = lax.rem(me, 2)
    way = 1 - 2 * parity
    far = lax.rem(me + 2 * way + count, count)
    far_back = lax.rem(me - 2 * way + count, count)
    near = lax.rem(me - way + count, count)
    mate = me + way

    barrier = pltpu.get_barrier_semaphore()
    for device in (far, far_back, near, mate):
        pl.semaphore_signal(
            barrier, inc=1, device_id=(device,), device_id_type=pl.DeviceIdType.MESH
        )

    def remote(source, target, sems, i, device):
        return pltpu.make_async_remote_copy(
            src_ref=source,
            dst_ref=target,
            send_sem=sems.at[0, i],
            recv_sem=sems.at[1, i],
            device_id=(device,),
            device_id_type=pl.DeviceIdType.MESH,
        )

    def frames(block, i):
        return all_ref.at[:, aligned(block + i * COLS, COLS)]

    def norms(block, i):
        return rn_ref.at[:, aligned(block + i * COLS, COLS)]

    def far_copies(i):
        return (
            remote(frames(OWN, i), frames(FAR, i), far_sems, i, far_back),
            remote(norms(OWN, i), norms(FAR, i), far_n_sems, i, far_back),
        )

    def near_copies(i):
        return (
            remote(frames(FAR, i), frames(NEAR, i), near_sems, i, mate),
            remote(norms(FAR, i), norms(NEAR, i), near_n_sems, i, mate),
        )

    def mate_copies(i):
        return (
            remote(frames(OWN, i), frames(MATE, i), mate_sems, i, mate),
            remote(norms(OWN, i), norms(MATE, i), mate_n_sems, i, mate),
        )

    def y_copy(row, half, sems, i, device):
        cols = aligned(half * HALF, HALF)
        source = y_ref.at[aligned(row, COLS), cols]
        return remote(source, got_ref.at[aligned(row - FAR, COLS), cols], sems, i, device)

    def far_y_copy(i):
        return y_copy(FAR + (i >> 1) * COLS, i & 1, far_y_sems, i, far)

    def near_y_copy(i):
        return y_copy(NEAR_OUT + (i & 1) * COLS, i >> 1, near_y_sems, i, near)

    def mate_y_copy(i):
        return y_copy(MATE_OUT + (i & 1) * COLS, i >> 1, mate_y_sems, i, mate)

    centre(x_ref, all_ref, own_ref, ln_ref, rn_ref)
    pl.semaphore_wait(barrier, 4)
    for i in range(CHUNKS):
        for copy in (*far_copies(i), *mate_copies(i)):
            copy.start()

    def take(group):
        @pl.when((group >= FAR_AT - 1) & (group < NEAR_AT - 1) & ((group & 1) == (FAR_AT - 1) % 2))
        def _():
            i = (group - FAR_AT + 1) >> 1
            for copy in far_copies(i):
                copy.wait_recv()
            for copy in near_copies(i):
                copy.start()

        @pl.when(group == NEAR_AT - 1)
        def _():
            for i in range(CHUNKS):
                for copy in near_copies(i):
                    copy.wait_recv()

        @pl.when(group == MATE_AT - 1)
        def _():
            for i in range(CHUNKS):
                for copy in mate_copies(i):
                    copy.wait_recv()

    def give(group):
        @pl.when((group > FAR_AT) & (group <= NEAR_AT))
        def _():
            far_y_copy(group - FAR_AT - 1).start()

        @pl.when((group > NEAR_AT) & (group <= MATE_AT))
        def _():
            near_y_copy(group - NEAR_AT - 1).start()

        @pl.when(group > MATE_AT)
        def _():
            mate_y_copy(group - MATE_AT - 1).start()

    def turn(row, _, out, old):
        y_ref[aligned(out, COLS), aligned(row, ROWS)] = old[...].T

    def step(last, now, following, cov, cov_next, old, old_last):
        row, col, out = now
        products = covariance_pieces(all_ref, *following[:2], cov_next)
        pieces = value_pieces(cov, ln_ref, rn_ref, row, col)
        for _, (r, values) in interleave(pieces, products):
            tile[aligned(row + r, STEP), aligned(out, COLS)] = values
            old[r : r + STEP, :] = encode(values)
        turn(*last, old_last)

    first = group_place(jnp.int32(0), parity)
    for _ in covariance_pieces(all_ref, *first[:2], cov0):
        pass
    old1[...] = jnp.zeros_like(old1)

    def body(group, places):
        last, now = places
        second = second_place(group, now)
        following = group_place(jnp.minimum(group + 1, GROUPS - 1), parity)
        step(last, now, second, cov0, cov1, old0, old1)
        take(group)
        give(group)
        step(now, second, following, cov1, cov0, old1, old0)
        return second, following

    last, _ = lax.fori_loop(0, GROUPS, body, (first, first))
    turn(*last, old1)
    mate_y_copy(CHUNKS - 1).start()

    for i in range(CHUNKS):
        for copy in (*far_copies(i), *mate_copies(i), *near_copies(i)):
            copy.wait_send()
        near_y_copy(i).wait()
        mate_y_copy(i).wait()
    for i in range(2 * CHUNKS):
        far_y_copy(i).wait()


def main(coords, count):
    pair = pltpu.SemaphoreType.DMA((2, CHUNKS))
    pairs = [pair] * 9
    pairs[3] = pltpu.SemaphoreType.DMA((2, 2 * CHUNKS))
    return pl.pallas_call(
        functools.partial(main_kernel, count),
        in_specs=[VMEM],
        out_specs=[VMEM] * 6,
        out_shape=[
            jax.ShapeDtypeStruct((FR, WIDTH), jnp.float32),
            jax.ShapeDtypeStruct((WIDTH, FR), jnp.bfloat16),
            jax.ShapeDtypeStruct((WIDTH - FR, FR), jnp.bfloat16),
            jax.ShapeDtypeStruct((3, FR, ATOMS), jnp.bfloat16),
            jax.ShapeDtypeStruct((FR, 128), jnp.float32),
            jax.ShapeDtypeStruct((8, 4 * FR), jnp.float32),
        ],
        scratch_shapes=[
            pltpu.VMEM((3, 4 * FR, ATOMS), jnp.bfloat16),
            pltpu.VMEM((3, 3, ROWS, COLS), jnp.float32),
            pltpu.VMEM((3, 3, ROWS, COLS), jnp.float32),
            pltpu.VMEM((ROWS, COLS), jnp.bfloat16),
            pltpu.VMEM((ROWS, COLS), jnp.bfloat16),
            *pairs,
        ],
        compiler_params=pltpu.CompilerParams(
            collective_id=0, has_side_effects=True, vmem_limit_bytes=MAIN_LIMIT
        ),
        cost_estimate=pl.CostEstimate(
            flops=45 * FR * FR * ATOMS, bytes_accessed=32 << 20, transcendentals=0
        ),
        name="deviations",
    )(coords)


def decode(values):
    return lax.rsqrt(lax.rsqrt(values.astype(jnp.float32)))


def finish_kernel(
    tile, y_ref, got_ref, own_ref, ln_ref, rn_ref, out_ref,
    far_tile, rest_tile, low_tile, column, turned, cov0, cov1, old0, old1, sem,
):
    parity = lax.rem(lax.axis_index("frames"), 2)
    copies = []

    def copy(source, slot, rows, cols, start=True):
        copies.append(
            pltpu.make_async_copy(source, out_ref.at[slot, rows, cols], sem.at[len(copies)])
        )
        if start:
            copies[-1].start()
        return copies[-1]

    def half(i):
        return aligned(i * HALF, HALF)

    both, last = pl.ds(0, FR), pl.ds(LAST, COLS)
    near_slot, near_flip = near_place(parity)
    mate_slot, mate_flip = mate_place(parity)
    quarters = (
        (NEAR_OUT, near_slot, near_flip, rest_tile.at[0]),
        (MATE_OUT, mate_slot, mate_flip, rest_tile.at[1]),
    )
    copy(tile.at[:, pl.ds(FAR, FR)], 4 * (1 - parity), both, both)
    for first, slot, flip, _ in quarters:
        for i in range(2):
            other = half(other_half(i, flip))
            copy(tile.at[half(i), pl.ds(first, HALF)], slot, half(i), other)
    for c in range(CHUNKS - 1):
        rows, cols = pl.ds(0, (c + 1) * COLS), pl.ds(c * COLS, COLS)
        copy(tile.at[rows, cols], 2, rows, cols)

    far_copies = [
        copy(far_tile.at[half(i)], 4 * parity, half(i), both, start=False) for i in range(2)
    ]
    quarter_copies = [
        [
            copy(tiles.at[:, half(i)], slot, half(other_half(i, 1 - flip)), half(i), start=False)
            for i in range(2)
        ]
        for _, slot, flip, tiles in quarters
    ]
    column_copies = [copy(column.at[half(i)], 2, half(i), last, start=False) for i in range(2)]
    low_copies = []
    for c in range(1, CHUNKS - 1):
        low, cols = pl.ds(c * COLS, COLS), pl.ds(0, c * COLS)
        low_copies.append(copy(low_tile.at[low, cols], 2, low, cols, start=False))
    turned_copy = copy(turned, 2, last, pl.ds(0, LAST), start=False)

    def turn(row, old):
        turned[:, aligned(row, ROWS)] = old[...].T

    def step(row, row_last, row_next, cov, cov_next, old, old_last, also):
        products = covariance_pieces(own_ref, row_next, LAST, cov_next)
        pieces = value_pieces(cov, ln_ref, rn_ref, row, LAST)
        for piece, (r, values) in interleave(pieces, products):
            column[aligned(row + r, STEP), :] = values
            old[r : r + STEP, :] = values
            also(piece)
        turn(row_last, old_last)

    for _ in covariance_pieces(own_ref, 0, LAST, cov0):
        pass
    old1[...] = jnp.zeros_like(old1)

    def decode_far(i, piece):
        rows = aligned(i * HALF + piece * 32, 32)
        far_tile[rows, :] = decode(got_ref[rows, :])

    def decode_rest(i, piece):
        rows, low = pl.ds(piece * 32, 32), aligned(COLS + i * COLS + piece * 16, 16)
        near_or_mate = aligned(NEAR_OUT - FAR + i * HALF + piece * 32, 32)
        rest_tile[i, rows, :] = decode(got_ref[near_or_mate, :])
        low_tile[low, :] = decode(y_ref[low, 0:HALF])

    completed = (
        (far_copies[0],),
        (*quarter_copies[0], column_copies[0], low_copies[0]),
        (far_copies[1],),
        (*quarter_copies[1], column_copies[1], low_copies[1]),
    )

    @pl.loop(0, len(completed))
    def _(s):
        row = s * ROWS
        places = row, jnp.maximum(row - ROWS, 0), jnp.minimum(row + ROWS, LAST)

        @pl.when((s & 1) == 0)
        def _():
            step(*places, cov0, cov1, old0, old1, functools.partial(decode_far, s >> 1))

        @pl.when((s & 1) == 1)
        def _():
            step(*places, cov1, cov0, old1, old0, functools.partial(decode_rest, s >> 1))

        for each, group in enumerate(completed):

            @pl.when(s == each)
            def _():
                for piece in group:
                    piece.start()

    turned_copy.start()
    for each in copies:
        each.wait()


def finish(*held):
    return pl.pallas_call(
        finish_kernel,
        in_specs=[ANY] + [VMEM] * 5,
        out_specs=ANY,
        out_shape=jax.ShapeDtypeStruct((5, FR, FR), jnp.float32),
        scratch_shapes=[
            pltpu.VMEM((FR, FR), jnp.float32),
            pltpu.VMEM((2, HALF, FR), jnp.float32),
            pltpu.VMEM((LAST, HALF), jnp.float32),
            pltpu.VMEM((FR, COLS), jnp.float32),
            pltpu.VMEM((COLS, LAST), jnp.float32),
            pltpu.VMEM((3, 3, ROWS, COLS), jnp.float32),
            pltpu.VMEM((3, 3, ROWS, COLS), jnp.float32),
            pltpu.VMEM((ROWS, COLS), jnp.float32),
            pltpu.VMEM((ROWS, COLS), jnp.float32),
            pltpu.SemaphoreType.DMA((32,)),
        ],
        compiler_params=pltpu.CompilerParams(vmem_limit_bytes=FINISH_LIMIT),
        name="finish",
    )(*held)


def on_device(coords):
    out = finish(*main(coords, lax.axis_size("frames")))
    return jnp.transpose(out, (1, 0, 2))


def solution(mesh):
    return jax.shard_map(
        on_device,
        mesh=mesh,
        in_specs=(P(None, "frames", None),),
        out_specs=P("frames", None, None),
        check_vma=False,
    )
```

```python
import functools

import jax
import jax.numpy as jnp
from jax import lax
from jax.experimental import pallas as pl
from jax.experimental.pallas import tpu as pltpu
from jax.sharding import PartitionSpec as P

NEWTON = 8
FR = 1024
ATOMS = 256
ROWS = 256
COLS = 256
STEP = 16
HALF = FR // 2
VMEM = pl.BlockSpec(memory_space=pltpu.VMEM)
ANY = pl.BlockSpec(memory_space=pl.ANY)
MAIN_LIMIT = 12 << 20
FINISH_LIMIT = 22 << 20


def aligned(index, size):
    if isinstance(index, int):
        return pl.ds(index, size)
    return pl.ds(pl.multiple_of(index, size), size)


def centre(x_ref, all_ref, own_ref, ln_ref, rn_ref, first):
    weights = jnp.full((ATOMS, 128), 1.0 / ATOMS, jnp.bfloat16)

    @pl.loop(0, COLS // 128)
    def _(i):
        rows = aligned(first + i * 128, 128)
        total = None
        for k in range(3):
            values = x_ref[k, rows, :]
            mean = jnp.dot(values, weights, preferred_element_type=jnp.float32)
            mean = jnp.concatenate([mean] * (ATOMS // 128), axis=1)
            centred = (values.astype(jnp.float32) - mean).astype(jnp.bfloat16)
            all_ref[k, rows, :] = centred
            own_ref[k, rows, :] = centred
            back = centred.astype(jnp.float32)
            total = back * back if total is None else total + back * back
        norms = jnp.broadcast_to(0.5 * jnp.sum(total, axis=1, keepdims=True), (128, 128))
        ln_ref[rows, :] = norms
        rn_ref[:, rows] = norms.T[0:8, :]


def invariants(entry):
    (a, b, c), (d, f, g), (h, i, j) = entry
    first = a * a + b * b + c * c
    others = (d * d + f * f + g * g) + (h * h + i * i + j * j)
    p = f * j - g * i
    q = g * h - d * j
    r = d * i - f * h
    det = a * p + b * q + c * r
    one = a * d + b * f + c * g
    two = a * h + b * i + c * j
    minors = (first * others - one * one - two * two) + (p * p + q * q + r * r)
    return first + others, det + det, minors


def deviations(entry, left, right):
    n, f, m = invariants(entry)
    start = left + right
    top = start
    for _ in range(NEWTON):
        h = top * top - n
        top = ((h * 0.75 + n) * h + m) * pltpu.reciprocal(top * h - f, approx=True)
    return (start - top) * (2.0 / ATOMS)


def covariance_pieces(all_ref, row, col, cov_ref):
    left = all_ref[:, aligned(row, ROWS), :].reshape(3 * ROWS, ATOMS)
    for k in range(3):
        right = all_ref[k, aligned(col, COLS), :]
        block = lax.dot_general(
            left, right, (((1,), (1,)), ((), ())), preferred_element_type=jnp.float32
        )
        cov_ref[:, k] = block.reshape(3, ROWS, COLS)
        yield


def interleave(values, products):
    for piece, value in enumerate(values):
        yield piece, value
        if piece in (2, 8, 13):
            next(products, None)


def value_pieces(cov_ref, ln_ref, rn_ref, row, col):
    for r in range(0, ROWS, STEP):
        entry = [[cov_ref[k, l, r : r + STEP, :] for l in range(3)] for k in range(3)]
        left = ln_ref[aligned(row + r, STEP), :]
        left = jnp.concatenate([left] * (COLS // 128), axis=1)
        right = rn_ref[:, aligned(col, COLS)]
        right = jnp.concatenate([right] * (STEP // 8), axis=0)
        yield r, deviations(entry, left, right)


def encode(values):
    square = values * values
    return (square * square).astype(jnp.bfloat16)


def other_half(half, flip):
    return half + flip - 2 * half * flip


def mate_place(parity):
    return 3 - 2 * parity, parity


def near_place(parity):
    return 1 + 2 * parity, 1 - parity


OWN, FAR, NEAR, MATE = range(0, 4 * FR, FR)
NEAR_OUT, MATE_OUT, WIDTH = 2 * FR, 2 * FR + HALF, 3 * FR
FAR_AT, NEAR_AT, MATE_AT, GROUPS = 4, 12, 16, 20
SPLIT = 2
CHUNKS = FR // COLS
LAST = FR - COLS


def group_place(g, parity):
    row = jnp.where(g == SPLIT, 2, 0)
    col = jnp.where(g == 0, 1, jnp.where(g <= SPLIT, 2, 3)) * COLS

    far = g - FAR_AT
    is_far = g >= FAR_AT
    row = jnp.where(is_far, (far & 1) * 2, row)
    col = jnp.where(is_far, FAR + (far >> 1) * COLS, col)

    inner = (g - NEAR_AT) & 3
    is_quarter, is_mate = g >= NEAR_AT, g >= MATE_AT
    flip = jnp.where(is_mate, parity, 1 - parity)
    half = inner >> 1
    row = jnp.where(is_quarter, half * 2, row)
    inside = (inner & 1) * COLS
    out = jnp.where(is_quarter, jnp.where(is_mate, MATE_OUT, NEAR_OUT) + inside, col)
    base = jnp.where(is_mate, MATE, NEAR) + inside
    col = jnp.where(is_quarter, base + other_half(half, flip) * HALF, col)
    return row * ROWS, col, out


def second_place(g, first):
    row, col, out = first
    return tuple(jnp.where(g == SPLIT, 0, each) for each in (row + ROWS, col, out))


def main_kernel(
    count, x_ref, tile, y_ref, got_ref, own_ref, ln_ref, rn_ref,
    all_ref, cov0, cov1, old0, old1,
    frame_sems, norm_sems, y_sems,
):
    me = lax.axis_index("frames")
    parity = lax.rem(me, 2)
    way = 1 - 2 * parity
    far = lax.rem(me + 2 * way + count, count)
    far_back = lax.rem(me - 2 * way + count, count)
    near = lax.rem(me - way + count, count)
    mate = me + way

    barrier = pltpu.get_barrier_semaphore()
    for device in (far, far_back, near, mate):
        pl.semaphore_signal(
            barrier, inc=1, device_id=(device,), device_id_type=pl.DeviceIdType.MESH
        )

    def remote(source, target, sems, i, device):
        return pltpu.make_async_remote_copy(
            src_ref=source,
            dst_ref=target,
            send_sem=sems.at[0, i],
            recv_sem=sems.at[1, i],
            device_id=(device,),
            device_id_type=pl.DeviceIdType.MESH,
        )

    def frames(block, i):
        return all_ref.at[:, aligned(block + i * COLS, COLS)]

    def norms(block, i):
        return rn_ref.at[:, aligned(block + i * COLS, COLS)]

    def frame_copies(k):
        i, kind = k & 3, k >> 2
        source = jnp.where(kind == 1, FAR, OWN)
        target = jnp.where(kind == 0, FAR, jnp.where(kind == 1, NEAR, MATE))
        device = jnp.where(kind == 0, far_back, mate)
        return (
            remote(frames(source, i), frames(target, i), frame_sems, k, device),
            remote(norms(source, i), norms(target, i), norm_sems, k, device),
        )

    def y_copy(k):
        is_far = k < 8
        half = jnp.where(is_far, k & 1, (k >> 1) & 1)
        quarter = NEAR_OUT + ((k - 8) >> 2) * HALF + (k & 1) * COLS
        row = jnp.where(is_far, FAR + (k >> 1) * COLS, quarter)
        device = jnp.where(is_far, far, jnp.where(k < 12, near, mate))
        cols = aligned(half * HALF, HALF)
        source = y_ref.at[aligned(row, COLS), cols]
        return remote(source, got_ref.at[aligned(row - FAR, COLS), cols], y_sems, k, device)

    centre(x_ref, all_ref, own_ref, ln_ref, rn_ref, 0)
    pl.semaphore_wait(barrier, 4)
    for copy in frame_copies(jnp.int32(0)):
        copy.start()
    for i in range(1, CHUNKS):
        centre(x_ref, all_ref, own_ref, ln_ref, rn_ref, i * COLS)

    def between(group):
        @pl.when((group >= FAR_AT - 1) & (group < NEAR_AT - 2) & ((group & 1) == 1))
        def _():
            for copy in frame_copies((group - FAR_AT + 1) >> 1):
                copy.wait_recv()

        @pl.when((group >= NEAR_AT - 4) & (group < MATE_AT))
        def _():
            for copy in frame_copies(group - NEAR_AT + 8):
                copy.wait_recv()

        is_far = ((group & 1) == 1) & (group < 7)
        is_near = ((group & 1) == 0) & (group > 2)
        chunk = jnp.where(group == 2, 8, 8 + ((group - 5) >> 1))
        chunk = jnp.where(is_near, 4 + ((group - 4) >> 1), chunk)
        chunk = jnp.where(is_far, (group + 1) >> 1, chunk)

        @pl.when((group >= 1) & (group < NEAR_AT))
        def _():
            for copy in frame_copies(chunk):
                copy.start()

        @pl.when(group > FAR_AT)
        def _():
            y_copy(group - FAR_AT - 1).start()

    def turn(row, _, out, old):
        y_ref[aligned(out, COLS), aligned(row, ROWS)] = old[...].T

    def step(last, now, following, cov, cov_next, old, old_last):
        row, col, out = now
        products = covariance_pieces(all_ref, *following[:2], cov_next)
        pieces = value_pieces(cov, ln_ref, rn_ref, row, col)
        for _, (r, values) in interleave(pieces, products):
            tile[aligned(row + r, STEP), aligned(out, COLS)] = values
            old[r : r + STEP, :] = encode(values)
        turn(*last, old_last)

    first = group_place(jnp.int32(0), parity)
    for _ in covariance_pieces(all_ref, *first[:2], cov0):
        pass
    old1[...] = jnp.zeros_like(old1)

    def body(group, places):
        last, now = places
        second = second_place(group, now)
        following = group_place(jnp.minimum(group + 1, GROUPS - 1), parity)
        step(last, now, second, cov0, cov1, old0, old1)
        between(group)
        step(now, second, following, cov1, cov0, old1, old0)
        return second, following

    last, _ = lax.fori_loop(0, GROUPS, body, (first, first))
    turn(*last, old1)
    last_copy = GROUPS - FAR_AT - 1
    y_copy(jnp.int32(last_copy)).start()

    @pl.loop(0, 3 * CHUNKS)
    def _(k):
        for copy in frame_copies(k):
            copy.wait_send()

    @pl.loop(0, last_copy + 1)
    def _(k):
        y_copy(k).wait()


def main(coords, count):
    return pl.pallas_call(
        functools.partial(main_kernel, count),
        in_specs=[VMEM],
        out_specs=[VMEM] * 6,
        out_shape=[
            jax.ShapeDtypeStruct((FR, WIDTH), jnp.float32),
            jax.ShapeDtypeStruct((WIDTH, FR), jnp.bfloat16),
            jax.ShapeDtypeStruct((WIDTH - FR, FR), jnp.bfloat16),
            jax.ShapeDtypeStruct((3, FR, ATOMS), jnp.bfloat16),
            jax.ShapeDtypeStruct((FR, 128), jnp.float32),
            jax.ShapeDtypeStruct((8, 4 * FR), jnp.float32),
        ],
        scratch_shapes=[
            pltpu.VMEM((3, 4 * FR, ATOMS), jnp.bfloat16),
            pltpu.VMEM((3, 3, ROWS, COLS), jnp.float32),
            pltpu.VMEM((3, 3, ROWS, COLS), jnp.float32),
            pltpu.VMEM((ROWS, COLS), jnp.bfloat16),
            pltpu.VMEM((ROWS, COLS), jnp.bfloat16),
            pltpu.SemaphoreType.DMA((2, 3 * CHUNKS)),
            pltpu.SemaphoreType.DMA((2, 3 * CHUNKS)),
            pltpu.SemaphoreType.DMA((2, GROUPS - FAR_AT)),
        ],
        compiler_params=pltpu.CompilerParams(
            collective_id=0, has_side_effects=True, vmem_limit_bytes=MAIN_LIMIT
        ),
        cost_estimate=pl.CostEstimate(
            flops=45 * FR * FR * ATOMS, bytes_accessed=32 << 20, transcendentals=0
        ),
        name="deviations",
    )(coords)


def decode(values):
    return lax.rsqrt(lax.rsqrt(values.astype(jnp.float32)))


def finish_kernel(
    tile, y_ref, got_ref, own_ref, ln_ref, rn_ref, out_ref,
    far_tile, rest_tile, low_tile, column, turned, cov0, cov1, old0, old1, sem,
):
    parity = lax.rem(lax.axis_index("frames"), 2)
    copies = []

    def copy(source, slot, rows, cols, start=True):
        copies.append(
            pltpu.make_async_copy(source, out_ref.at[slot, rows, cols], sem.at[len(copies)])
        )
        if start:
            copies[-1].start()
        return copies[-1]

    def half(i):
        return aligned(i * HALF, HALF)

    both, last = pl.ds(0, FR), pl.ds(LAST, COLS)
    near_slot, near_flip = near_place(parity)
    mate_slot, mate_flip = mate_place(parity)
    quarters = (
        (NEAR_OUT, near_slot, near_flip, rest_tile.at[0]),
        (MATE_OUT, mate_slot, mate_flip, rest_tile.at[1]),
    )
    copy(tile.at[:, pl.ds(FAR, FR)], 4 * (1 - parity), both, both)
    for first, slot, flip, _ in quarters:
        for i in range(2):
            other = half(other_half(i, flip))
            copy(tile.at[half(i), pl.ds(first, HALF)], slot, half(i), other)
    for c in range(CHUNKS):
        rows, cols = pl.ds(0, HALF if c == CHUNKS - 1 else (c + 1) * COLS), pl.ds(c * COLS, COLS)
        copy(tile.at[rows, cols], 2, rows, cols)

    def later(source, slot, rows, cols):
        return copy(source, slot, rows, cols, start=False)

    first_rows, second_rows = pl.ds(HALF, COLS), pl.ds(LAST, COLS)
    far_copies = [later(far_tile.at[half(i)], 4 * parity, half(i), both) for i in range(2)]
    (near_copies, mate_copies) = (
        [later(tiles.at[:, half(i)], slot, half(other_half(i, 1 - flip)), half(i)) for i in range(2)]
        for _, slot, flip, tiles in quarters
    )
    completed = [
        [far_copies[0], *near_copies, later(column.at[pl.ds(0, COLS)], 2, first_rows, last)],
        [far_copies[1], *mate_copies, later(column.at[pl.ds(COLS, COLS)], 2, second_rows, last)],
    ]
    for c in range(1, CHUNKS):
        low, cols = pl.ds(c * COLS, COLS), pl.ds(0, min(c * COLS, HALF))
        completed[c > 1].append(later(low_tile.at[low, cols], 2, low, cols))
    completed[1].append(later(turned, 2, last, first_rows))

    def decode_pieces(s, piece):
        rows = aligned(s * HALF + piece * 32, 32)
        far_tile[rows, :] = decode(got_ref[rows, :])
        near_or_mate = aligned(NEAR_OUT - FAR + s * HALF + piece * 32, 32)
        rest_tile[s, pl.ds(piece * 32, 32), :] = decode(got_ref[near_or_mate, :])
        low = pl.ds(COLS + piece * 16, 16) if s == 0 else pl.ds(HALF + piece * 32, 32)
        low_tile[low, :] = decode(y_ref[low, 0:HALF])

    def step(s, cov, old, products):
        row = HALF + s * ROWS
        pieces = value_pieces(cov, ln_ref, rn_ref, row, LAST)
        for piece, (r, values) in interleave(pieces, products):
            column[s * ROWS + r : s * ROWS + r + STEP, :] = values
            old[r : r + STEP, :] = values
            decode_pieces(s, piece)

    for _ in covariance_pieces(own_ref, HALF, LAST, cov0):
        pass

    @pl.loop(0, 2)
    def _(s):
        @pl.when(s == 0)
        def _():
            step(0, cov0, old0, covariance_pieces(own_ref, LAST, LAST, cov1))

        @pl.when(s == 1)
        def _():
            step(1, cov1, old1, iter(()))
            turned[...] = old0[...].T

        for each, group in enumerate(completed):

            @pl.when(s == each)
            def _():
                for piece in group:
                    piece.start()

    for each in copies:
        each.wait()


def finish(*held):
    return pl.pallas_call(
        finish_kernel,
        in_specs=[ANY] + [VMEM] * 5,
        out_specs=ANY,
        out_shape=jax.ShapeDtypeStruct((5, FR, FR), jnp.float32),
        scratch_shapes=[
            pltpu.VMEM((FR, FR), jnp.float32),
            pltpu.VMEM((2, HALF, FR), jnp.float32),
            pltpu.VMEM((FR, HALF), jnp.float32),
            pltpu.VMEM((HALF, COLS), jnp.float32),
            pltpu.VMEM((COLS, COLS), jnp.float32),
            pltpu.VMEM((3, 3, ROWS, COLS), jnp.float32),
            pltpu.VMEM((3, 3, ROWS, COLS), jnp.float32),
            pltpu.VMEM((ROWS, COLS), jnp.float32),
            pltpu.VMEM((ROWS, COLS), jnp.float32),
            pltpu.SemaphoreType.DMA((32,)),
        ],
        compiler_params=pltpu.CompilerParams(vmem_limit_bytes=FINISH_LIMIT),
        name="finish",
    )(*held)


def on_device(coords):
    out = finish(*main(coords, lax.axis_size("frames")))
    return jnp.transpose(out, (1, 0, 2))


def solution(mesh):
    return jax.shard_map(
        on_device,
        mesh=mesh,
        in_specs=(P(None, "frames", None),),
        out_specs=P("frames", None, None),
        check_vma=False,
    )
```

```python
import functools

import jax
import jax.numpy as jnp
from jax import lax
from jax.experimental import pallas as pl
from jax.experimental.pallas import tpu as pltpu
from jax.sharding import PartitionSpec as P

NEWTON = 8
FR = 1024
ATOMS = 256
ROWS = 256
COLS = 256
STEP = 16
HALF = FR // 2
VMEM = pl.BlockSpec(memory_space=pltpu.VMEM)
ANY = pl.BlockSpec(memory_space=pl.ANY)
MAIN_LIMIT = 12 << 20
FINISH_LIMIT = 22 << 20


def aligned(index, size):
    if isinstance(index, int):
        return pl.ds(index, size)
    return pl.ds(pl.multiple_of(index, size), size)


def centre(x_ref, all_ref, own_ref, ln_ref, rn_ref, first):
    weights = jnp.full((ATOMS, 128), 1.0 / ATOMS, jnp.bfloat16)

    @pl.loop(0, COLS // 128)
    def _(i):
        rows = aligned(first + i * 128, 128)
        total = None
        for k in range(3):
            values = x_ref[k, rows, :]
            mean = jnp.dot(values, weights, preferred_element_type=jnp.float32)
            mean = jnp.concatenate([mean] * (ATOMS // 128), axis=1)
            centred = (values.astype(jnp.float32) - mean).astype(jnp.bfloat16)
            all_ref[k, rows, :] = centred
            own_ref[k, rows, :] = centred
            back = centred.astype(jnp.float32)
            total = back * back if total is None else total + back * back
        norms = jnp.broadcast_to(0.5 * jnp.sum(total, axis=1, keepdims=True), (128, 128))
        ln_ref[rows, :] = norms
        rn_ref[:, rows] = norms.T[0:8, :]


def invariants(entry):
    (a, b, c), (d, f, g), (h, i, j) = entry
    first = a * a + b * b + c * c
    others = (d * d + f * f + g * g) + (h * h + i * i + j * j)
    p = f * j - g * i
    q = g * h - d * j
    r = d * i - f * h
    det = a * p + b * q + c * r
    one = a * d + b * f + c * g
    two = a * h + b * i + c * j
    minors = (first * others - one * one - two * two) + (p * p + q * q + r * r)
    return first + others, det + det, minors


def deviations(entry, left, right):
    n, f, m = invariants(entry)
    start = left + right
    top = start
    for _ in range(NEWTON):
        h = top * top - n
        top = ((h * 0.75 + n) * h + m) * pltpu.reciprocal(top * h - f, approx=True)
    return (start - top) * (2.0 / ATOMS)


def covariance_pieces(all_ref, row, col, cov_ref):
    left = all_ref[:, aligned(row, ROWS), :].reshape(3 * ROWS, ATOMS)
    for k in range(3):
        right = all_ref[k, aligned(col, COLS), :]
        block = lax.dot_general(
            left, right, (((1,), (1,)), ((), ())), preferred_element_type=jnp.float32
        )
        cov_ref[:, k] = block.reshape(3, ROWS, COLS)
        yield


def interleave(values, products):
    for piece, value in enumerate(values):
        yield piece, value
        if piece in (2, 8, 13):
            next(products, None)


def value_pieces(cov_ref, ln_ref, rn_ref, row, col):
    for r in range(0, ROWS, STEP):
        entry = [[cov_ref[k, l, r : r + STEP, :] for l in range(3)] for k in range(3)]
        left = ln_ref[aligned(row + r, STEP), :]
        left = jnp.concatenate([left] * (COLS // 128), axis=1)
        right = rn_ref[:, aligned(col, COLS)]
        right = jnp.concatenate([right] * (STEP // 8), axis=0)
        yield r, deviations(entry, left, right)


def encode(values):
    square = values * values
    return (square * square).astype(jnp.bfloat16)


def other_half(half, flip):
    return half + flip - 2 * half * flip


def mate_place(parity):
    return 3 - 2 * parity, parity


def near_place(parity):
    return 1 + 2 * parity, 1 - parity


OWN, FAR, NEAR, MATE = range(0, 4 * FR, FR)
NEAR_OUT, MATE_OUT, WIDTH = 2 * FR, 2 * FR + HALF, 3 * FR
LAST_ROW = FR - ROWS
FAR_AT, NEAR_AT, EXTRA_AT, MATE_AT, GROUPS = 4, 12, 16, 17, 21
SPLIT = 2
EXTRA_ROW, SENDS = LAST_ROW, 15
CHUNKS = FR // COLS
LAST = FR - COLS


def group_place(g, parity):
    row = jnp.where(g == SPLIT, 2, 0)
    col = jnp.where(g == 0, 1, jnp.where(g <= SPLIT, 2, 3)) * COLS

    far = g - FAR_AT
    is_far = g >= FAR_AT
    row = jnp.where(is_far, (far & 1) * 2, row)
    col = jnp.where(is_far, FAR + (far >> 1) * COLS, col)

    is_quarter, is_mate = g >= NEAR_AT, g >= MATE_AT
    inner = (g - jnp.where(is_mate, MATE_AT, NEAR_AT)) & 3
    flip = jnp.where(is_mate, parity, 1 - parity)
    half = inner >> 1
    row = jnp.where(is_quarter, half * 2, row)
    inside = (inner & 1) * COLS
    out = jnp.where(is_quarter, jnp.where(is_mate, MATE_OUT, NEAR_OUT) + inside, col)
    base = jnp.where(is_mate, MATE, NEAR) + inside
    col = jnp.where(is_quarter, base + other_half(half, flip) * HALF, col)

    is_extra = g == EXTRA_AT
    out_row = jnp.where(is_extra, EXTRA_ROW, row * ROWS)
    row = jnp.where(is_extra, extra_row(parity), row * ROWS)
    return row, jnp.where(is_extra, NEAR + HALF, col), out_row, jnp.where(is_extra, 0, out)


def extra_row(parity):
    return other_half(1, parity) * HALF + COLS


def second_place(g, first):
    row, col, out_row, out = first
    is_extra = g == EXTRA_AT
    down, along = jnp.where(is_extra, 0, ROWS), jnp.where(is_extra, COLS, 0)
    second = row + down, col + along, out_row + down, out + along
    return tuple(jnp.where(g == SPLIT, 0, each) for each in second)


def main_kernel(
    count, x_ref, tile, y_ref, got_ref, own_ref, ln_ref, rn_ref,
    all_ref, cov0, cov1, old0, old1,
    frame_sems, norm_sems, y_sems,
):
    me = lax.axis_index("frames")
    parity = lax.rem(me, 2)
    way = 1 - 2 * parity
    far = lax.rem(me + 2 * way + count, count)
    far_back = lax.rem(me - 2 * way + count, count)
    near = lax.rem(me - way + count, count)
    mate = me + way

    barrier = pltpu.get_barrier_semaphore()
    for device in (far, far_back, near, mate):
        pl.semaphore_signal(
            barrier, inc=1, device_id=(device,), device_id_type=pl.DeviceIdType.MESH
        )

    def remote(source, target, sems, i, device):
        return pltpu.make_async_remote_copy(
            src_ref=source,
            dst_ref=target,
            send_sem=sems.at[0, i],
            recv_sem=sems.at[1, i],
            device_id=(device,),
            device_id_type=pl.DeviceIdType.MESH,
        )

    def frames(block, i):
        return all_ref.at[:, aligned(block + i * COLS, COLS)]

    def norms(block, i):
        return rn_ref.at[:, aligned(block + i * COLS, COLS)]

    def frame_copies(k):
        i, kind = k & 3, k >> 2
        source = jnp.where(kind == 1, FAR, OWN)
        target = jnp.where(kind == 0, FAR, jnp.where(kind == 1, NEAR, MATE))
        device = jnp.where(kind == 0, far_back, mate)
        return (
            remote(frames(source, i), frames(target, i), frame_sems, k, device),
            remote(norms(source, i), norms(target, i), norm_sems, k, device),
        )

    def y_copy(k):
        is_far, is_near = k < 8, k < 11
        i = k - jnp.where(is_near, 8, 11)
        half = jnp.where(is_far, k & 1, i >> 1)
        quarter = jnp.where(is_near, NEAR_OUT, MATE_OUT) + (i & 1) * COLS
        row = jnp.where(is_far, FAR + (k >> 1) * COLS, quarter)
        device = jnp.where(is_far, far, jnp.where(is_near, near, mate))
        cols = aligned(half * HALF, HALF)
        source = y_ref.at[aligned(row, COLS), cols]
        return remote(source, got_ref.at[aligned(row - FAR, COLS), cols], y_sems, k, device)

    centre(x_ref, all_ref, own_ref, ln_ref, rn_ref, 0)
    pl.semaphore_wait(barrier, 4)
    for copy in frame_copies(jnp.int32(0)):
        copy.start()
    for i in range(1, CHUNKS):
        centre(x_ref, all_ref, own_ref, ln_ref, rn_ref, i * COLS)

    def between(group):
        @pl.when((group >= FAR_AT - 1) & (group < NEAR_AT - 2) & ((group & 1) == 1))
        def _():
            for copy in frame_copies((group - FAR_AT + 1) >> 1):
                copy.wait_recv()

        @pl.when((group >= NEAR_AT - 4) & (group < NEAR_AT + 4))
        def _():
            for copy in frame_copies(group - NEAR_AT + 8):
                copy.wait_recv()

        is_odd = (group & 1) == 1
        chunk = jnp.where(is_odd, 9 + ((group - 5) >> 1), 4 + ((group - 4) >> 1))
        chunk = jnp.where(group < 4, jnp.where(group == 1, 8, jnp.maximum(group, 1)), chunk)

        @pl.when(group < NEAR_AT - 1)
        def _():
            for copy in frame_copies(chunk):
                copy.start()

        @pl.when((group > FAR_AT) & ((group < EXTRA_AT) | (group > MATE_AT)))
        def _():
            y_copy(group - FAR_AT - jnp.where(group < EXTRA_AT, 1, 3)).start()

    def turn(_, __, row, out, old):
        y_ref[aligned(out, COLS), aligned(row, ROWS)] = old[...].T

    def step(last, now, following, cov, cov_next, old, old_last):
        row, col, out_row, out = now
        products = covariance_pieces(all_ref, *following[:2], cov_next)
        pieces = value_pieces(cov, ln_ref, rn_ref, row, col)
        for _, (r, values) in interleave(pieces, products):
            tile[aligned(out_row + r, STEP), aligned(out, COLS)] = values
            old[r : r + STEP, :] = encode(values)
        turn(*last, old_last)

    first = group_place(jnp.int32(0), parity)
    for _ in covariance_pieces(all_ref, *first[:2], cov0):
        pass
    old1[...] = jnp.zeros_like(old1)

    def body(group, places):
        last, now = places
        second = second_place(group, now)
        following = group_place(jnp.minimum(group + 1, GROUPS - 1), parity)
        step(last, now, second, cov0, cov1, old0, old1)
        between(group)
        step(now, second, following, cov1, cov0, old1, old0)
        return second, following

    last, _ = lax.fori_loop(0, GROUPS, body, (first, first))
    turn(*last, old1)
    y_copy(jnp.int32(SENDS - 1)).start()

    @pl.loop(0, 3 * CHUNKS)
    def _(k):
        for copy in frame_copies(k):
            copy.wait_send()

    @pl.loop(0, SENDS)
    def _(k):
        y_copy(k).wait()


def main(coords, count):
    return pl.pallas_call(
        functools.partial(main_kernel, count),
        in_specs=[VMEM],
        out_specs=[VMEM] * 6,
        out_shape=[
            jax.ShapeDtypeStruct((FR, WIDTH), jnp.float32),
            jax.ShapeDtypeStruct((WIDTH, FR), jnp.bfloat16),
            jax.ShapeDtypeStruct((WIDTH - FR, FR), jnp.bfloat16),
            jax.ShapeDtypeStruct((3, FR, ATOMS), jnp.bfloat16),
            jax.ShapeDtypeStruct((FR, 128), jnp.float32),
            jax.ShapeDtypeStruct((8, 4 * FR), jnp.float32),
        ],
        scratch_shapes=[
            pltpu.VMEM((3, 4 * FR, ATOMS), jnp.bfloat16),
            pltpu.VMEM((3, 3, ROWS, COLS), jnp.float32),
            pltpu.VMEM((3, 3, ROWS, COLS), jnp.float32),
            pltpu.VMEM((ROWS, COLS), jnp.bfloat16),
            pltpu.VMEM((ROWS, COLS), jnp.bfloat16),
            pltpu.SemaphoreType.DMA((2, 3 * CHUNKS)),
            pltpu.SemaphoreType.DMA((2, 3 * CHUNKS)),
            pltpu.SemaphoreType.DMA((2, SENDS)),
        ],
        compiler_params=pltpu.CompilerParams(
            collective_id=0, has_side_effects=True, vmem_limit_bytes=MAIN_LIMIT
        ),
        cost_estimate=pl.CostEstimate(
            flops=45 * FR * FR * ATOMS, bytes_accessed=32 << 20, transcendentals=0
        ),
        name="deviations",
    )(coords)


def decode(values):
    return lax.rsqrt(lax.rsqrt(values.astype(jnp.float32)))


def finish_kernel(
    tile, y_ref, got_ref, own_ref, ln_ref, rn_ref, out_ref,
    far_tile, rest_tile, low_tile, column, turned, cov0, cov1, old0, old1, sem,
):
    parity = lax.rem(lax.axis_index("frames"), 2)
    copies = []

    def copy(source, slot, rows, cols, start=True):
        copies.append(
            pltpu.make_async_copy(source, out_ref.at[slot, rows, cols], sem.at[len(copies)])
        )
        if start:
            copies[-1].start()
        return copies[-1]

    def half(i):
        return aligned(i * HALF, HALF)

    both, last = pl.ds(0, FR), pl.ds(LAST, COLS)
    near_slot, near_flip = near_place(parity)
    mate_slot, mate_flip = mate_place(parity)
    quarters = (
        (NEAR_OUT, near_slot, near_flip, rest_tile.at[0]),
        (MATE_OUT, mate_slot, mate_flip, rest_tile.at[1]),
    )
    copy(tile.at[:, pl.ds(FAR, FR)], 4 * (1 - parity), both, both)
    for first, slot, flip, _ in quarters:
        for i in range(2):
            other = half(other_half(i, flip))
            copy(tile.at[half(i), pl.ds(first, HALF)], slot, half(i), other)
    for c in range(CHUNKS):
        rows, cols = pl.ds(0, HALF if c == CHUNKS - 1 else (c + 1) * COLS), pl.ds(c * COLS, COLS)
        copy(tile.at[rows, cols], 2, rows, cols)

    extra_rows = aligned(extra_row(parity), ROWS)
    extra = tile.at[pl.ds(EXTRA_ROW, ROWS), pl.ds(0, HALF)]
    copy(extra, near_slot, extra_rows, pl.ds(HALF, HALF))

    def later(source, slot, rows, cols):
        return copy(source, slot, rows, cols, start=False)

    first_rows, second_rows = pl.ds(HALF, COLS), pl.ds(LAST, COLS)
    far_copies = [later(far_tile.at[half(i)], 4 * parity, half(i), both) for i in range(2)]
    def quarter_copy(block, i, rows):
        _, slot, flip, tiles = quarters[block]
        target = aligned(other_half(i, 1 - flip) * HALF, rows)
        return later(tiles.at[pl.ds(0, rows), half(i)], slot, target, half(i))

    near_copies = [quarter_copy(0, 0, HALF), quarter_copy(0, 1, HALF - COLS)]
    mate_copies = [quarter_copy(1, 0, HALF), quarter_copy(1, 1, HALF)]
    completed = [
        [far_copies[0], *near_copies, later(column.at[pl.ds(0, COLS)], 2, first_rows, last)],
        [far_copies[1], *mate_copies, later(column.at[pl.ds(COLS, COLS)], 2, second_rows, last)],
    ]
    for c in range(1, CHUNKS):
        low, cols = pl.ds(c * COLS, COLS), pl.ds(0, min(c * COLS, HALF))
        completed[c > 1].append(later(low_tile.at[low, cols], 2, low, cols))
    completed[1].append(later(turned, 2, last, first_rows))

    def decode_pieces(s, piece):
        rows = aligned(s * HALF + piece * 32, 32)
        far_tile[rows, :] = decode(got_ref[rows, :])
        near_or_mate = aligned(NEAR_OUT - FAR + s * HALF + piece * 32, 32)
        rest_tile[s, pl.ds(piece * 32, 32), :] = decode(got_ref[near_or_mate, :])
        low = pl.ds(COLS + piece * 16, 16) if s == 0 else pl.ds(HALF + piece * 32, 32)
        low_tile[low, :] = decode(y_ref[low, 0:HALF])

    def step(s, cov, old, products):
        row = HALF + s * ROWS
        pieces = value_pieces(cov, ln_ref, rn_ref, row, LAST)
        for piece, (r, values) in interleave(pieces, products):
            column[s * ROWS + r : s * ROWS + r + STEP, :] = values
            old[r : r + STEP, :] = values
            decode_pieces(s, piece)

    for _ in covariance_pieces(own_ref, HALF, LAST, cov0):
        pass

    @pl.loop(0, 2)
    def _(s):
        @pl.when(s == 0)
        def _():
            step(0, cov0, old0, covariance_pieces(own_ref, LAST, LAST, cov1))

        @pl.when(s == 1)
        def _():
            step(1, cov1, old1, iter(()))
            turned[...] = old0[...].T

        for each, group in enumerate(completed):

            @pl.when(s == each)
            def _():
                for piece in group:
                    piece.start()

    for each in copies:
        each.wait()


def finish(*held):
    return pl.pallas_call(
        finish_kernel,
        in_specs=[ANY] + [VMEM] * 5,
        out_specs=ANY,
        out_shape=jax.ShapeDtypeStruct((5, FR, FR), jnp.float32),
        scratch_shapes=[
            pltpu.VMEM((FR, FR), jnp.float32),
            pltpu.VMEM((2, HALF, FR), jnp.float32),
            pltpu.VMEM((FR, HALF), jnp.float32),
            pltpu.VMEM((HALF, COLS), jnp.float32),
            pltpu.VMEM((COLS, COLS), jnp.float32),
            pltpu.VMEM((3, 3, ROWS, COLS), jnp.float32),
            pltpu.VMEM((3, 3, ROWS, COLS), jnp.float32),
            pltpu.VMEM((ROWS, COLS), jnp.float32),
            pltpu.VMEM((ROWS, COLS), jnp.float32),
            pltpu.SemaphoreType.DMA((32,)),
        ],
        compiler_params=pltpu.CompilerParams(vmem_limit_bytes=FINISH_LIMIT),
        name="finish",
    )(*held)


def on_device(coords):
    out = finish(*main(coords, lax.axis_size("frames")))
    return jnp.transpose(out, (1, 0, 2))


def solution(mesh):
    return jax.shard_map(
        on_device,
        mesh=mesh,
        in_specs=(P(None, "frames", None),),
        out_specs=P("frames", None, None),
        check_vma=False,
    )
```

```python
import functools

import jax
import jax.numpy as jnp
from jax import lax
from jax.experimental import pallas as pl
from jax.experimental.pallas import tpu as pltpu
from jax.sharding import PartitionSpec as P

NEWTON = 8
FR = 1024
ATOMS = 256
ROWS = 256
COLS = 256
STEP = 16
HALF = FR // 2
VMEM = pl.BlockSpec(memory_space=pltpu.VMEM)
ANY = pl.BlockSpec(memory_space=pl.ANY)
MAIN_LIMIT = 12 << 20
FINISH_LIMIT = 22 << 20


def aligned(index, size):
    if isinstance(index, int):
        return pl.ds(index, size)
    return pl.ds(pl.multiple_of(index, size), size)


def centre(x_ref, all_ref, own_ref, ln_ref, rn_ref, first):
    weights = jnp.full((ATOMS, 128), 1.0 / ATOMS, jnp.bfloat16)

    @pl.loop(0, COLS // 128)
    def _(i):
        rows = aligned(first + i * 128, 128)
        total = None
        for k in range(3):
            values = x_ref[k, rows, :]
            mean = jnp.dot(values, weights, preferred_element_type=jnp.float32)
            mean = jnp.concatenate([mean] * (ATOMS // 128), axis=1)
            centred = (values.astype(jnp.float32) - mean).astype(jnp.bfloat16)
            all_ref[k, rows, :] = centred
            own_ref[k, rows, :] = centred
            back = centred.astype(jnp.float32)
            total = back * back if total is None else total + back * back
        norms = jnp.broadcast_to(0.5 * jnp.sum(total, axis=1, keepdims=True), (128, 128))
        ln_ref[rows, :] = norms
        rn_ref[:, rows] = norms.T[0:8, :]


def invariants(entry):
    (a, b, c), (d, f, g), (h, i, j) = entry
    first = a * a + b * b + c * c
    others = (d * d + f * f + g * g) + (h * h + i * i + j * j)
    p = f * j - g * i
    q = g * h - d * j
    r = d * i - f * h
    det = a * p + b * q + c * r
    one = a * d + b * f + c * g
    two = a * h + b * i + c * j
    minors = (first * others - one * one - two * two) + (p * p + q * q + r * r)
    return first + others, det + det, minors


def deviations(entry, left, right):
    n, f, m = invariants(entry)
    start = left + right
    top = start
    for _ in range(NEWTON):
        h = top * top - n
        top = ((h * 0.75 + n) * h + m) * pltpu.reciprocal(top * h - f, approx=True)
    return (start - top) * (2.0 / ATOMS)


def covariance_pieces(all_ref, row, col, cov_ref):
    left = all_ref[:, aligned(row, ROWS), :].reshape(3 * ROWS, ATOMS)
    for k in range(3):
        right = all_ref[k, aligned(col, COLS), :]
        block = lax.dot_general(
            left, right, (((1,), (1,)), ((), ())), preferred_element_type=jnp.float32
        )
        cov_ref[:, k] = block.reshape(3, ROWS, COLS)
        yield


def interleave(values, products):
    for piece, value in enumerate(values):
        yield piece, value
        if piece in (2, 8, 13):
            next(products, None)


def value_pieces(cov_ref, ln_ref, rn_ref, row, col):
    for r in range(0, ROWS, STEP):
        entry = [[cov_ref[k, l, r : r + STEP, :] for l in range(3)] for k in range(3)]
        left = ln_ref[aligned(row + r, STEP), :]
        left = jnp.concatenate([left] * (COLS // 128), axis=1)
        right = rn_ref[:, aligned(col, COLS)]
        right = jnp.concatenate([right] * (STEP // 8), axis=0)
        yield r, deviations(entry, left, right)


def encode(values):
    square = values * values
    return (square * square).astype(jnp.bfloat16)


def other_half(half, flip):
    return half + flip - 2 * half * flip


def mate_place(parity):
    return 3 - 2 * parity, parity


def near_place(parity):
    return 1 + 2 * parity, 1 - parity


OWN, FAR, NEAR, MATE = range(0, 4 * FR, FR)
NEAR_OUT, MATE_OUT, WIDTH = 2 * FR, 2 * FR + HALF, 3 * FR
FAR_AT, NEAR_AT, MATE_AT, GROUPS = 4, 12, 16, 20
SPLIT = 2
CHUNKS = FR // COLS
LAST = FR - COLS


def group_place(g, parity):
    row = jnp.where(g == SPLIT, 2, 0)
    col = jnp.where(g == 0, 1, jnp.where(g <= SPLIT, 2, 3)) * COLS

    far = g - FAR_AT
    is_far = g >= FAR_AT
    row = jnp.where(is_far, (far & 1) * 2, row)
    col = jnp.where(is_far, FAR + (far >> 1) * COLS, col)

    inner = (g - NEAR_AT) & 3
    is_quarter, is_mate = g >= NEAR_AT, g >= MATE_AT
    flip = jnp.where(is_mate, parity, 1 - parity)
    half = inner >> 1
    row = jnp.where(is_quarter, half * 2, row)
    inside = (inner & 1) * COLS
    out = jnp.where(is_quarter, jnp.where(is_mate, MATE_OUT, NEAR_OUT) + inside, col)
    base = jnp.where(is_mate, MATE, NEAR) + inside
    col = jnp.where(is_quarter, base + other_half(half, flip) * HALF, col)
    return row * ROWS, col, out


def second_place(g, first):
    row, col, out = first
    return tuple(jnp.where(g == SPLIT, 0, each) for each in (row + ROWS, col, out))


def main_kernel(
    count, x_ref, tile, y_ref, got_ref, own_ref, ln_ref, rn_ref,
    all_ref, cov0, cov1, old0, old1,
    frame_sems, norm_sems, y_sems,
):
    me = lax.axis_index("frames")
    parity = lax.rem(me, 2)
    way = 1 - 2 * parity
    far = lax.rem(me + 2 * way + count, count)
    far_back = lax.rem(me - 2 * way + count, count)
    near = lax.rem(me - way + count, count)
    mate = me + way

    barrier = pltpu.get_barrier_semaphore()
    for device in (far, far_back, near, mate):
        pl.semaphore_signal(
            barrier, inc=1, device_id=(device,), device_id_type=pl.DeviceIdType.MESH
        )

    def remote(source, target, sems, i, device):
        return pltpu.make_async_remote_copy(
            src_ref=source,
            dst_ref=target,
            send_sem=sems.at[0, i],
            recv_sem=sems.at[1, i],
            device_id=(device,),
            device_id_type=pl.DeviceIdType.MESH,
        )

    def frames(block, i):
        return all_ref.at[:, aligned(block + i * COLS, COLS)]

    def norms(block, i):
        return rn_ref.at[:, aligned(block + i * COLS, COLS)]

    def frame_copies(k):
        i, kind = k & 3, k >> 2
        source = jnp.where(kind == 1, FAR, OWN)
        target = jnp.where(kind == 0, FAR, jnp.where(kind == 1, NEAR, MATE))
        device = jnp.where(kind == 0, far_back, mate)
        return (
            remote(frames(source, i), frames(target, i), frame_sems, k, device),
            remote(norms(source, i), norms(target, i), norm_sems, k, device),
        )

    def y_copy(k):
        is_far = k < 8
        half = jnp.where(is_far, k & 1, (k >> 1) & 1)
        quarter = NEAR_OUT + ((k - 8) >> 2) * HALF + (k & 1) * COLS
        row = jnp.where(is_far, FAR + (k >> 1) * COLS, quarter)
        device = jnp.where(is_far, far, jnp.where(k < 12, near, mate))
        cols = aligned(half * HALF, HALF)
        source = y_ref.at[aligned(row, COLS), cols]
        return remote(source, got_ref.at[aligned(row - FAR, COLS), cols], y_sems, k, device)

    for i in range(CHUNKS):
        centre(x_ref, all_ref, own_ref, ln_ref, rn_ref, i * COLS)
    pl.semaphore_wait(barrier, 4)
    for copy in frame_copies(jnp.int32(0)):
        copy.start()

    def between(group):
        @pl.when((group >= FAR_AT - 1) & (group < NEAR_AT - 2) & ((group & 1) == 1))
        def _():
            for copy in frame_copies((group - FAR_AT + 1) >> 1):
                copy.wait_recv()

        @pl.when((group >= NEAR_AT - 4) & (group < MATE_AT))
        def _():
            for copy in frame_copies(group - NEAR_AT + 8):
                copy.wait_recv()

        is_odd = (group & 1) == 1
        chunk = jnp.where(is_odd, 9 + ((group - 5) >> 1), 4 + ((group - 4) >> 1))
        chunk = jnp.where(group < 4, jnp.where(group == 1, 8, jnp.maximum(group, 1)), chunk)

        @pl.when(group < NEAR_AT - 1)
        def _():
            for copy in frame_copies(chunk):
                copy.start()

        @pl.when(group > FAR_AT)
        def _():
            y_copy(group - FAR_AT - 1).start()

    def turn(row, _, out, old):
        y_ref[aligned(out, COLS), aligned(row, ROWS)] = old[...].T

    def step(last, now, following, cov, cov_next, old, old_last):
        row, col, out = now
        products = covariance_pieces(all_ref, *following[:2], cov_next)
        pieces = value_pieces(cov, ln_ref, rn_ref, row, col)
        for _, (r, values) in interleave(pieces, products):
            tile[aligned(row + r, STEP), aligned(out, COLS)] = values
            old[r : r + STEP, :] = encode(values)
        turn(*last, old_last)

    first = group_place(jnp.int32(0), parity)
    for _ in covariance_pieces(all_ref, *first[:2], cov0):
        pass
    old1[...] = jnp.zeros_like(old1)

    def body(group, places):
        last, now = places
        second = second_place(group, now)
        following = group_place(jnp.minimum(group + 1, GROUPS - 1), parity)
        step(last, now, second, cov0, cov1, old0, old1)
        between(group)
        step(now, second, following, cov1, cov0, old1, old0)
        return second, following

    last, _ = lax.fori_loop(0, GROUPS, body, (first, first))
    turn(*last, old1)
    last_copy = GROUPS - FAR_AT - 1
    y_copy(jnp.int32(last_copy)).start()

    @pl.loop(0, 3 * CHUNKS)
    def _(k):
        for copy in frame_copies(k):
            copy.wait_send()

    @pl.loop(0, last_copy + 1)
    def _(k):
        y_copy(k).wait()


def main(coords, count):
    return pl.pallas_call(
        functools.partial(main_kernel, count),
        in_specs=[VMEM],
        out_specs=[VMEM] * 6,
        out_shape=[
            jax.ShapeDtypeStruct((FR, WIDTH), jnp.float32),
            jax.ShapeDtypeStruct((WIDTH, FR), jnp.bfloat16),
            jax.ShapeDtypeStruct((WIDTH - FR, FR), jnp.bfloat16),
            jax.ShapeDtypeStruct((3, FR, ATOMS), jnp.bfloat16),
            jax.ShapeDtypeStruct((FR, 128), jnp.float32),
            jax.ShapeDtypeStruct((8, 4 * FR), jnp.float32),
        ],
        scratch_shapes=[
            pltpu.VMEM((3, 4 * FR, ATOMS), jnp.bfloat16),
            pltpu.VMEM((3, 3, ROWS, COLS), jnp.float32),
            pltpu.VMEM((3, 3, ROWS, COLS), jnp.float32),
            pltpu.VMEM((ROWS, COLS), jnp.bfloat16),
            pltpu.VMEM((ROWS, COLS), jnp.bfloat16),
            pltpu.SemaphoreType.DMA((2, 3 * CHUNKS)),
            pltpu.SemaphoreType.DMA((2, 3 * CHUNKS)),
            pltpu.SemaphoreType.DMA((2, GROUPS - FAR_AT)),
        ],
        compiler_params=pltpu.CompilerParams(
            collective_id=0, has_side_effects=True, vmem_limit_bytes=MAIN_LIMIT
        ),
        cost_estimate=pl.CostEstimate(
            flops=45 * FR * FR * ATOMS, bytes_accessed=32 << 20, transcendentals=0
        ),
        name="deviations",
    )(coords)


def decode(values):
    return lax.rsqrt(lax.rsqrt(values.astype(jnp.float32)))


def finish_kernel(
    tile, y_ref, got_ref, own_ref, ln_ref, rn_ref, out_ref,
    far_tile, rest_tile, low_tile, column, turned, cov0, cov1, old0, old1, sem,
):
    parity = lax.rem(lax.axis_index("frames"), 2)
    copies = []

    def copy(source, slot, rows, cols, start=True):
        copies.append(
            pltpu.make_async_copy(source, out_ref.at[slot, rows, cols], sem.at[len(copies)])
        )
        if start:
            copies[-1].start()
        return copies[-1]

    def half(i):
        return aligned(i * HALF, HALF)

    both, last = pl.ds(0, FR), pl.ds(LAST, COLS)
    near_slot, near_flip = near_place(parity)
    mate_slot, mate_flip = mate_place(parity)
    quarters = (
        (NEAR_OUT, near_slot, near_flip, rest_tile.at[0]),
        (MATE_OUT, mate_slot, mate_flip, rest_tile.at[1]),
    )
    copy(tile.at[:, pl.ds(FAR, FR)], 4 * (1 - parity), both, both)
    for first, slot, flip, _ in quarters:
        for i in range(2):
            other = half(other_half(i, flip))
            copy(tile.at[half(i), pl.ds(first, HALF)], slot, half(i), other)
    for c in range(CHUNKS):
        rows, cols = pl.ds(0, HALF if c == CHUNKS - 1 else (c + 1) * COLS), pl.ds(c * COLS, COLS)
        copy(tile.at[rows, cols], 2, rows, cols)

    def later(source, slot, rows, cols):
        return copy(source, slot, rows, cols, start=False)

    first_rows, second_rows = pl.ds(HALF, COLS), pl.ds(LAST, COLS)
    far_copies = [later(far_tile.at[half(i)], 4 * parity, half(i), both) for i in range(2)]
    (near_copies, mate_copies) = (
        [later(tiles.at[:, half(i)], slot, half(other_half(i, 1 - flip)), half(i)) for i in range(2)]
        for _, slot, flip, tiles in quarters
    )
    completed = [
        [far_copies[0], *near_copies, later(column.at[pl.ds(0, COLS)], 2, first_rows, last)],
        [far_copies[1], *mate_copies, later(column.at[pl.ds(COLS, COLS)], 2, second_rows, last)],
    ]
    for c in range(1, CHUNKS):
        low, cols = pl.ds(c * COLS, COLS), pl.ds(0, min(c * COLS, HALF))
        completed[c > 1].append(later(low_tile.at[low, cols], 2, low, cols))
    completed[1].append(later(turned, 2, last, first_rows))

    def decode_pieces(s, piece):
        rows = aligned(s * HALF + piece * 32, 32)
        far_tile[rows, :] = decode(got_ref[rows, :])
        near_or_mate = aligned(NEAR_OUT - FAR + s * HALF + piece * 32, 32)
        rest_tile[s, pl.ds(piece * 32, 32), :] = decode(got_ref[near_or_mate, :])
        low = pl.ds(COLS + piece * 16, 16) if s == 0 else pl.ds(HALF + piece * 32, 32)
        low_tile[low, :] = decode(y_ref[low, 0:HALF])

    def step(s, cov, old, products):
        row = HALF + s * ROWS
        pieces = value_pieces(cov, ln_ref, rn_ref, row, LAST)
        for piece, (r, values) in interleave(pieces, products):
            column[s * ROWS + r : s * ROWS + r + STEP, :] = values
            old[r : r + STEP, :] = values
            decode_pieces(s, piece)

    for _ in covariance_pieces(own_ref, HALF, LAST, cov0):
        pass

    @pl.loop(0, 2)
    def _(s):
        @pl.when(s == 0)
        def _():
            step(0, cov0, old0, covariance_pieces(own_ref, LAST, LAST, cov1))

        @pl.when(s == 1)
        def _():
            step(1, cov1, old1, iter(()))
            turned[...] = old0[...].T

        for each, group in enumerate(completed):

            @pl.when(s == each)
            def _():
                for piece in group:
                    piece.start()

    for each in copies:
        each.wait()


def finish(*held):
    return pl.pallas_call(
        finish_kernel,
        in_specs=[ANY] + [VMEM] * 5,
        out_specs=ANY,
        out_shape=jax.ShapeDtypeStruct((5, FR, FR), jnp.float32),
        scratch_shapes=[
            pltpu.VMEM((FR, FR), jnp.float32),
            pltpu.VMEM((2, HALF, FR), jnp.float32),
            pltpu.VMEM((FR, HALF), jnp.float32),
            pltpu.VMEM((HALF, COLS), jnp.float32),
            pltpu.VMEM((COLS, COLS), jnp.float32),
            pltpu.VMEM((3, 3, ROWS, COLS), jnp.float32),
            pltpu.VMEM((3, 3, ROWS, COLS), jnp.float32),
            pltpu.VMEM((ROWS, COLS), jnp.float32),
            pltpu.VMEM((ROWS, COLS), jnp.float32),
            pltpu.SemaphoreType.DMA((32,)),
        ],
        compiler_params=pltpu.CompilerParams(vmem_limit_bytes=FINISH_LIMIT),
        name="finish",
    )(*held)


def on_device(coords):
    out = finish(*main(coords, lax.axis_size("frames")))
    return jnp.transpose(out, (1, 0, 2))


def solution(mesh):
    return jax.shard_map(
        on_device,
        mesh=mesh,
        in_specs=(P(None, "frames", None),),
        out_specs=P("frames", None, None),
        check_vma=False,
    )
```

```python
import functools

import jax
import jax.numpy as jnp
from jax import lax
from jax.experimental import pallas as pl
from jax.experimental.pallas import tpu as pltpu
from jax.sharding import PartitionSpec as P

NEWTON = 8
FR = 1024
ATOMS = 256
ROWS = 256
COLS = 256
STEP = 16
HALF = FR // 2
VMEM = pl.BlockSpec(memory_space=pltpu.VMEM)
ANY = pl.BlockSpec(memory_space=pl.ANY)
MAIN_LIMIT = 12 << 20
FINISH_LIMIT = 22 << 20


def aligned(index, size):
    if isinstance(index, int):
        return pl.ds(index, size)
    return pl.ds(pl.multiple_of(index, size), size)


def centre(x_ref, all_ref, own_ref, ln_ref, rn_ref, first):
    weights = jnp.full((ATOMS, 128), 1.0 / ATOMS, jnp.bfloat16)

    @pl.loop(0, COLS // 128)
    def _(i):
        rows = aligned(first + i * 128, 128)
        total = None
        for k in range(3):
            values = x_ref[k, rows, :]
            mean = jnp.dot(values, weights, preferred_element_type=jnp.float32)
            mean = jnp.concatenate([mean] * (ATOMS // 128), axis=1)
            centred = (values.astype(jnp.float32) - mean).astype(jnp.bfloat16)
            all_ref[k, rows, :] = centred
            own_ref[k, rows, :] = centred
            back = centred.astype(jnp.float32)
            total = back * back if total is None else total + back * back
        norms = jnp.broadcast_to(0.5 * jnp.sum(total, axis=1, keepdims=True), (128, 128))
        ln_ref[rows, :] = norms
        rn_ref[:, rows] = norms.T[0:8, :]


def invariants(entry):
    (a, b, c), (d, f, g), (h, i, j) = entry
    first = a * a + b * b + c * c
    others = (d * d + f * f + g * g) + (h * h + i * i + j * j)
    p = f * j - g * i
    q = g * h - d * j
    r = d * i - f * h
    det = a * p + b * q + c * r
    one = a * d + b * f + c * g
    two = a * h + b * i + c * j
    minors = (first * others - one * one - two * two) + (p * p + q * q + r * r)
    return first + others, det + det, minors


def deviations(entry, left, right):
    n, f, m = invariants(entry)
    start = left + right
    top = start
    for _ in range(NEWTON):
        h = top * top - n
        top = ((h * 0.75 + n) * h + m) * pltpu.reciprocal(top * h - f, approx=True)
    return (start - top) * (2.0 / ATOMS)


def covariance_pieces(all_ref, row, col, cov_ref):
    left = all_ref[:, aligned(row, ROWS), :].reshape(3 * ROWS, ATOMS)
    for k in range(3):
        right = all_ref[k, aligned(col, COLS), :]
        block = lax.dot_general(
            left, right, (((1,), (1,)), ((), ())), preferred_element_type=jnp.float32
        )
        cov_ref[:, k] = block.reshape(3, ROWS, COLS)
        yield


def interleave(values, products):
    for piece, value in enumerate(values):
        yield piece, value
        if piece in (2, 8, 13):
            next(products, None)


def value_pieces(cov_ref, ln_ref, rn_ref, row, col):
    for r in range(0, ROWS, STEP):
        entry = [[cov_ref[k, l, r : r + STEP, :] for l in range(3)] for k in range(3)]
        left = ln_ref[aligned(row + r, STEP), :]
        left = jnp.concatenate([left] * (COLS // 128), axis=1)
        right = rn_ref[:, aligned(col, COLS)]
        right = jnp.concatenate([right] * (STEP // 8), axis=0)
        yield r, deviations(entry, left, right)


def encode(values):
    square = values * values
    return (square * square).astype(jnp.bfloat16)


def other_half(half, flip):
    return half + flip - 2 * half * flip


def mate_place(parity):
    return 3 - 2 * parity, parity


def near_place(parity):
    return 1 + 2 * parity, 1 - parity


OWN, FAR, NEAR, MATE = range(0, 4 * FR, FR)
NEAR_OUT, MATE_OUT, WIDTH = 2 * FR, 2 * FR + HALF, 3 * FR
FAR_AT, NEAR_AT, MATE_AT, GROUPS = 4, 12, 16, 20
SPLIT = 2
CHUNKS = FR // COLS
LAST = FR - COLS


def group_place(g, parity):
    row = jnp.where(g == SPLIT, 2, 0)
    col = jnp.where(g == 0, 1, jnp.where(g <= SPLIT, 2, 3)) * COLS

    far = g - FAR_AT
    is_far = g >= FAR_AT
    row = jnp.where(is_far, (far & 1) * 2, row)
    col = jnp.where(is_far, FAR + (far >> 1) * COLS, col)

    inner = (g - NEAR_AT) & 3
    is_quarter, is_mate = g >= NEAR_AT, g >= MATE_AT
    flip = jnp.where(is_mate, parity, 1 - parity)
    half = inner >> 1
    row = jnp.where(is_quarter, half * 2, row)
    inside = (inner & 1) * COLS
    out = jnp.where(is_quarter, jnp.where(is_mate, MATE_OUT, NEAR_OUT) + inside, col)
    base = jnp.where(is_mate, MATE, NEAR) + inside
    col = jnp.where(is_quarter, base + other_half(half, flip) * HALF, col)
    return row * ROWS, col, out


def second_place(g, first):
    row, col, out = first
    return tuple(jnp.where(g == SPLIT, 0, each) for each in (row + ROWS, col, out))


def main_kernel(
    count, x_ref, tile, y_ref, got_ref, own_ref, ln_ref, rn_ref,
    all_ref, cov0, cov1, old0, old1,
    frame_sems, norm_sems, y_sems,
):
    me = lax.axis_index("frames")
    parity = lax.rem(me, 2)
    way = 1 - 2 * parity
    far = lax.rem(me + 2 * way + count, count)
    far_back = lax.rem(me - 2 * way + count, count)
    near = lax.rem(me - way + count, count)
    mate = me + way

    barrier = pltpu.get_barrier_semaphore()
    for device in (far, mate):
        pl.semaphore_signal(
            barrier, inc=1, device_id=(device,), device_id_type=pl.DeviceIdType.MESH
        )

    def remote(source, target, sems, i, device):
        return pltpu.make_async_remote_copy(
            src_ref=source,
            dst_ref=target,
            send_sem=sems.at[0, i],
            recv_sem=sems.at[1, i],
            device_id=(device,),
            device_id_type=pl.DeviceIdType.MESH,
        )

    def frames(block, i):
        return all_ref.at[:, aligned(block + i * COLS, COLS)]

    def norms(block, i):
        return rn_ref.at[:, aligned(block + i * COLS, COLS)]

    def frame_copies(k):
        i, kind = k & 3, k >> 2
        source = jnp.where(kind == 1, FAR, OWN)
        target = jnp.where(kind == 0, FAR, jnp.where(kind == 1, NEAR, MATE))
        device = jnp.where(kind == 0, far_back, mate)
        return (
            remote(frames(source, i), frames(target, i), frame_sems, k, device),
            remote(norms(source, i), norms(target, i), norm_sems, k, device),
        )

    def y_copy(k):
        is_far = k < 8
        half = jnp.where(is_far, k & 1, (k >> 1) & 1)
        quarter = NEAR_OUT + ((k - 8) >> 2) * HALF + (k & 1) * COLS
        row = jnp.where(is_far, FAR + (k >> 1) * COLS, quarter)
        device = jnp.where(is_far, far, jnp.where(k < 12, near, mate))
        cols = aligned(half * HALF, HALF)
        source = y_ref.at[aligned(row, COLS), cols]
        return remote(source, got_ref.at[aligned(row - FAR, COLS), cols], y_sems, k, device)

    for i in range(CHUNKS):
        centre(x_ref, all_ref, own_ref, ln_ref, rn_ref, i * COLS)
    pl.semaphore_wait(barrier, 2)
    for copy in frame_copies(jnp.int32(0)):
        copy.start()

    def between(group):
        @pl.when((group >= FAR_AT - 1) & (group < NEAR_AT - 2) & ((group & 1) == 1))
        def _():
            for copy in frame_copies((group - FAR_AT + 1) >> 1):
                copy.wait_recv()

        @pl.when((group >= NEAR_AT - 4) & (group < MATE_AT))
        def _():
            for copy in frame_copies(group - NEAR_AT + 8):
                copy.wait_recv()

        is_odd = (group & 1) == 1
        chunk = jnp.where(is_odd, 9 + ((group - 5) >> 1), 4 + ((group - 4) >> 1))
        chunk = jnp.where(group < 4, jnp.where(group == 1, 8, jnp.maximum(group, 1)), chunk)

        @pl.when(group < NEAR_AT - 1)
        def _():
            for copy in frame_copies(chunk):
                copy.start()

        @pl.when(group > FAR_AT)
        def _():
            y_copy(group - FAR_AT - 1).start()

    def turn(row, _, out, old):
        y_ref[aligned(out, COLS), aligned(row, ROWS)] = old[...].T

    def step(last, now, following, cov, cov_next, old, old_last):
        row, col, out = now
        products = covariance_pieces(all_ref, *following[:2], cov_next)
        pieces = value_pieces(cov, ln_ref, rn_ref, row, col)
        for _, (r, values) in interleave(pieces, products):
            tile[aligned(row + r, STEP), aligned(out, COLS)] = values
            old[r : r + STEP, :] = encode(values)
        turn(*last, old_last)

    first = group_place(jnp.int32(0), parity)
    for _ in covariance_pieces(all_ref, *first[:2], cov0):
        pass
    old1[...] = jnp.zeros_like(old1)

    def body(group, places):
        last, now = places
        second = second_place(group, now)
        following = group_place(jnp.minimum(group + 1, GROUPS - 1), parity)
        step(last, now, second, cov0, cov1, old0, old1)
        between(group)
        step(now, second, following, cov1, cov0, old1, old0)
        return second, following

    last, _ = lax.fori_loop(0, GROUPS, body, (first, first))
    turn(*last, old1)
    last_copy = GROUPS - FAR_AT - 1
    y_copy(jnp.int32(last_copy)).start()

    @pl.loop(0, 3 * CHUNKS)
    def _(k):
        for copy in frame_copies(k):
            copy.wait_send()

    @pl.loop(0, last_copy + 1)
    def _(k):
        y_copy(k).wait()


def main(coords, count):
    return pl.pallas_call(
        functools.partial(main_kernel, count),
        in_specs=[VMEM],
        out_specs=[VMEM] * 6,
        out_shape=[
            jax.ShapeDtypeStruct((FR, WIDTH), jnp.float32),
            jax.ShapeDtypeStruct((WIDTH, FR), jnp.bfloat16),
            jax.ShapeDtypeStruct((WIDTH - FR, FR), jnp.bfloat16),
            jax.ShapeDtypeStruct((3, FR, ATOMS), jnp.bfloat16),
            jax.ShapeDtypeStruct((FR, 128), jnp.float32),
            jax.ShapeDtypeStruct((8, 4 * FR), jnp.float32),
        ],
        scratch_shapes=[
            pltpu.VMEM((3, 4 * FR, ATOMS), jnp.bfloat16),
            pltpu.VMEM((3, 3, ROWS, COLS), jnp.float32),
            pltpu.VMEM((3, 3, ROWS, COLS), jnp.float32),
            pltpu.VMEM((ROWS, COLS), jnp.bfloat16),
            pltpu.VMEM((ROWS, COLS), jnp.bfloat16),
            pltpu.SemaphoreType.DMA((2, 3 * CHUNKS)),
            pltpu.SemaphoreType.DMA((2, 3 * CHUNKS)),
            pltpu.SemaphoreType.DMA((2, GROUPS - FAR_AT)),
        ],
        compiler_params=pltpu.CompilerParams(
            collective_id=0, has_side_effects=True, vmem_limit_bytes=MAIN_LIMIT
        ),
        cost_estimate=pl.CostEstimate(
            flops=45 * FR * FR * ATOMS, bytes_accessed=32 << 20, transcendentals=0
        ),
        name="deviations",
    )(coords)


def decode(values):
    return lax.rsqrt(lax.rsqrt(values.astype(jnp.float32)))


def finish_kernel(
    tile, y_ref, got_ref, own_ref, ln_ref, rn_ref, out_ref,
    far_tile, rest_tile, low_tile, column, turned, cov0, cov1, old0, old1, sem,
):
    parity = lax.rem(lax.axis_index("frames"), 2)
    copies = []

    def copy(source, slot, rows, cols, start=True):
        copies.append(
            pltpu.make_async_copy(source, out_ref.at[slot, rows, cols], sem.at[len(copies)])
        )
        if start:
            copies[-1].start()
        return copies[-1]

    def half(i):
        return aligned(i * HALF, HALF)

    both, last = pl.ds(0, FR), pl.ds(LAST, COLS)
    near_slot, near_flip = near_place(parity)
    mate_slot, mate_flip = mate_place(parity)
    quarters = (
        (NEAR_OUT, near_slot, near_flip, rest_tile.at[0]),
        (MATE_OUT, mate_slot, mate_flip, rest_tile.at[1]),
    )
    copy(tile.at[:, pl.ds(FAR, FR)], 4 * (1 - parity), both, both)
    for first, slot, flip, _ in quarters:
        for i in range(2):
            other = half(other_half(i, flip))
            copy(tile.at[half(i), pl.ds(first, HALF)], slot, half(i), other)
    for c in range(CHUNKS):
        rows, cols = pl.ds(0, HALF if c == CHUNKS - 1 else (c + 1) * COLS), pl.ds(c * COLS, COLS)
        copy(tile.at[rows, cols], 2, rows, cols)

    def later(source, slot, rows, cols):
        return copy(source, slot, rows, cols, start=False)

    first_rows, second_rows = pl.ds(HALF, COLS), pl.ds(LAST, COLS)
    far_copies = [later(far_tile.at[half(i)], 4 * parity, half(i), both) for i in range(2)]
    (near_copies, mate_copies) = (
        [later(tiles.at[:, half(i)], slot, half(other_half(i, 1 - flip)), half(i)) for i in range(2)]
        for _, slot, flip, tiles in quarters
    )
    completed = [
        [far_copies[0], *near_copies, later(column.at[pl.ds(0, COLS)], 2, first_rows, last)],
        [far_copies[1], *mate_copies, later(column.at[pl.ds(COLS, COLS)], 2, second_rows, last)],
    ]
    for c in range(1, CHUNKS):
        low, cols = pl.ds(c * COLS, COLS), pl.ds(0, min(c * COLS, HALF))
        completed[c > 1].append(later(low_tile.at[low, cols], 2, low, cols))
    completed[1].append(later(turned, 2, last, first_rows))

    def decode_pieces(s, piece):
        rows = aligned(s * HALF + piece * 32, 32)
        far_tile[rows, :] = decode(got_ref[rows, :])
        near_or_mate = aligned(NEAR_OUT - FAR + s * HALF + piece * 32, 32)
        rest_tile[s, pl.ds(piece * 32, 32), :] = decode(got_ref[near_or_mate, :])
        low = pl.ds(COLS + piece * 16, 16) if s == 0 else pl.ds(HALF + piece * 32, 32)
        low_tile[low, :] = decode(y_ref[low, 0:HALF])

    def step(s, cov, old, products):
        row = HALF + s * ROWS
        pieces = value_pieces(cov, ln_ref, rn_ref, row, LAST)
        for piece, (r, values) in interleave(pieces, products):
            column[s * ROWS + r : s * ROWS + r + STEP, :] = values
            old[r : r + STEP, :] = values
            decode_pieces(s, piece)

    for _ in covariance_pieces(own_ref, HALF, LAST, cov0):
        pass

    @pl.loop(0, 2)
    def _(s):
        @pl.when(s == 0)
        def _():
            step(0, cov0, old0, covariance_pieces(own_ref, LAST, LAST, cov1))

        @pl.when(s == 1)
        def _():
            step(1, cov1, old1, iter(()))
            turned[...] = old0[...].T

        for each, group in enumerate(completed):

            @pl.when(s == each)
            def _():
                for piece in group:
                    piece.start()

    for each in copies:
        each.wait()


def finish(*held):
    return pl.pallas_call(
        finish_kernel,
        in_specs=[ANY] + [VMEM] * 5,
        out_specs=ANY,
        out_shape=jax.ShapeDtypeStruct((5, FR, FR), jnp.float32),
        scratch_shapes=[
            pltpu.VMEM((FR, FR), jnp.float32),
            pltpu.VMEM((2, HALF, FR), jnp.float32),
            pltpu.VMEM((FR, HALF), jnp.float32),
            pltpu.VMEM((HALF, COLS), jnp.float32),
            pltpu.VMEM((COLS, COLS), jnp.float32),
            pltpu.VMEM((3, 3, ROWS, COLS), jnp.float32),
            pltpu.VMEM((3, 3, ROWS, COLS), jnp.float32),
            pltpu.VMEM((ROWS, COLS), jnp.float32),
            pltpu.VMEM((ROWS, COLS), jnp.float32),
            pltpu.SemaphoreType.DMA((32,)),
        ],
        compiler_params=pltpu.CompilerParams(vmem_limit_bytes=FINISH_LIMIT),
        name="finish",
    )(*held)


def on_device(coords):
    out = finish(*main(coords, lax.axis_size("frames")))
    return jnp.transpose(out, (1, 0, 2))


def solution(mesh):
    return jax.shard_map(
        on_device,
        mesh=mesh,
        in_specs=(P(None, "frames", None),),
        out_specs=P("frames", None, None),
        check_vma=False,
    )
```

```python
import functools

import jax
import jax.numpy as jnp
from jax import lax
from jax.experimental import pallas as pl
from jax.experimental.pallas import tpu as pltpu
from jax.sharding import PartitionSpec as P

NEWTON = 8
FR = 1024
ATOMS = 256
ROWS = 256
COLS = 256
STEP = 16
HALF = FR // 2
VMEM = pl.BlockSpec(memory_space=pltpu.VMEM)
ANY = pl.BlockSpec(memory_space=pl.ANY)
MAIN_LIMIT = 12 << 20
FINISH_LIMIT = 22 << 20


def aligned(index, size):
    if isinstance(index, int):
        return pl.ds(index, size)
    return pl.ds(pl.multiple_of(index, size), size)


def centre(x_ref, all_ref, own_ref, ln_ref, rn_ref, first):
    weights = jnp.full((ATOMS, 128), 1.0 / ATOMS, jnp.bfloat16)

    @pl.loop(0, COLS // 128)
    def _(i):
        rows = aligned(first + i * 128, 128)
        total = None
        for k in range(3):
            values = x_ref[k, rows, :]
            mean = jnp.dot(values, weights, preferred_element_type=jnp.float32)
            mean = jnp.concatenate([mean] * (ATOMS // 128), axis=1)
            centred = (values.astype(jnp.float32) - mean).astype(jnp.bfloat16)
            all_ref[k, rows, :] = centred
            own_ref[k, rows, :] = centred
            back = centred.astype(jnp.float32)
            total = back * back if total is None else total + back * back
        norms = jnp.broadcast_to(0.5 * jnp.sum(total, axis=1, keepdims=True), (128, 128))
        ln_ref[rows, :] = norms
        rn_ref[:, rows] = norms.T[0:8, :]


def invariants(entry):
    (a, b, c), (d, f, g), (h, i, j) = entry
    first = a * a + b * b + c * c
    others = (d * d + f * f + g * g) + (h * h + i * i + j * j)
    p = f * j - g * i
    q = g * h - d * j
    r = d * i - f * h
    det = a * p + b * q + c * r
    one = a * d + b * f + c * g
    two = a * h + b * i + c * j
    minors = (first * others - one * one - two * two) + (p * p + q * q + r * r)
    return first + others, det + det, minors


def deviations(entry, left, right):
    n, f, m = invariants(entry)
    start = left + right
    top = start
    for _ in range(NEWTON):
        h = top * top - n
        top = ((h * 0.75 + n) * h + m) * pltpu.reciprocal(top * h - f, approx=True)
    return (start - top) * (2.0 / ATOMS)


def covariance_pieces(all_ref, row, col, cov_ref):
    left = all_ref[:, aligned(row, ROWS), :].reshape(3 * ROWS, ATOMS)
    for k in range(3):
        right = all_ref[k, aligned(col, COLS), :]
        block = lax.dot_general(
            left, right, (((1,), (1,)), ((), ())), preferred_element_type=jnp.float32
        )
        cov_ref[:, k] = block.reshape(3, ROWS, COLS)
        yield


def interleave(values, products):
    for piece, value in enumerate(values):
        yield piece, value
        if piece in (2, 8, 13):
            next(products, None)


def value_pieces(cov_ref, ln_ref, rn_ref, row, col):
    for r in range(0, ROWS, STEP):
        entry = [[cov_ref[k, l, r : r + STEP, :] for l in range(3)] for k in range(3)]
        left = ln_ref[aligned(row + r, STEP), :]
        left = jnp.concatenate([left] * (COLS // 128), axis=1)
        right = rn_ref[:, aligned(col, COLS)]
        right = jnp.concatenate([right] * (STEP // 8), axis=0)
        yield r, deviations(entry, left, right)


def encode(values):
    square = values * values
    return (square * square).astype(jnp.bfloat16)


def other_half(half, flip):
    return half + flip - 2 * half * flip


def mate_place(parity):
    return 3 - 2 * parity, parity


def near_place(parity):
    return 1 + 2 * parity, 1 - parity


OWN, FAR, NEAR, MATE = range(0, 4 * FR, FR)
NEAR_OUT, MATE_OUT, WIDTH = 2 * FR, 2 * FR + HALF, 3 * FR
FAR_AT, NEAR_AT, MATE_AT, GROUPS = 4, 12, 16, 20
SPLIT = 2
CHUNKS = FR // COLS
LAST = FR - COLS


def group_place(g, parity):
    row = jnp.where(g == SPLIT, 2, 0)
    col = jnp.where(g == 0, 1, jnp.where(g <= SPLIT, 2, 3)) * COLS

    far = g - FAR_AT
    is_far = g >= FAR_AT
    row = jnp.where(is_far, (far & 1) * 2, row)
    col = jnp.where(is_far, FAR + (far >> 1) * COLS, col)

    inner = (g - NEAR_AT) & 3
    is_quarter, is_mate = g >= NEAR_AT, g >= MATE_AT
    flip = jnp.where(is_mate, parity, 1 - parity)
    half = inner >> 1
    row = jnp.where(is_quarter, half * 2, row)
    inside = (inner & 1) * COLS
    out = jnp.where(is_quarter, jnp.where(is_mate, MATE_OUT, NEAR_OUT) + inside, col)
    base = jnp.where(is_mate, MATE, NEAR) + inside
    col = jnp.where(is_quarter, base + other_half(half, flip) * HALF, col)
    return row * ROWS, col, out


def second_place(g, first):
    row, col, out = first
    return tuple(jnp.where(g == SPLIT, 0, each) for each in (row + ROWS, col, out))


def main_kernel(
    count, x_ref, tile, y_ref, got_ref, own_ref, ln_ref, rn_ref,
    all_ref, cov0, cov1, old0, old1,
    frame_sems, norm_sems, y_sems,
):
    me = lax.axis_index("frames")
    parity = lax.rem(me, 2)
    way = 1 - 2 * parity
    far = lax.rem(me + 2 * way + count, count)
    far_back = lax.rem(me - 2 * way + count, count)
    near = lax.rem(me - way + count, count)
    mate = me + way

    barrier = pltpu.get_barrier_semaphore()
    for device in (far, mate):
        pl.semaphore_signal(
            barrier, inc=1, device_id=(device,), device_id_type=pl.DeviceIdType.MESH
        )

    def remote(source, target, sems, i, device):
        return pltpu.make_async_remote_copy(
            src_ref=source,
            dst_ref=target,
            send_sem=sems.at[0, i],
            recv_sem=sems.at[1, i],
            device_id=(device,),
            device_id_type=pl.DeviceIdType.MESH,
        )

    def frames(block, i):
        return all_ref.at[:, aligned(block + i * COLS, COLS)]

    def norms(block, i):
        return rn_ref.at[:, aligned(block + i * COLS, COLS)]

    def frame_copies(k):
        i, kind = k & 3, k >> 2
        source = jnp.where(kind == 1, FAR, OWN)
        target = jnp.where(kind == 0, FAR, jnp.where(kind == 1, NEAR, MATE))
        device = jnp.where(kind == 0, far_back, mate)
        return (
            remote(frames(source, i), frames(target, i), frame_sems, k, device),
            remote(norms(source, i), norms(target, i), norm_sems, k, device),
        )

    def y_copy(k):
        is_far = k < 8
        half = jnp.where(is_far, k & 1, (k >> 1) & 1)
        quarter = NEAR_OUT + ((k - 8) >> 2) * HALF + (k & 1) * COLS
        row = jnp.where(is_far, FAR + (k >> 1) * COLS, quarter)
        device = jnp.where(is_far, far, jnp.where(k < 12, near, mate))
        cols = aligned(half * HALF, HALF)
        source = y_ref.at[aligned(row, COLS), cols]
        return remote(source, got_ref.at[aligned(row - FAR, COLS), cols], y_sems, k, device)

    for i in range(CHUNKS):
        centre(x_ref, all_ref, own_ref, ln_ref, rn_ref, i * COLS)
    pl.semaphore_wait(barrier, 2)
    for copy in frame_copies(jnp.int32(0)):
        copy.start()

    def between(group):
        @pl.when((group >= FAR_AT - 1) & (group < NEAR_AT - 2) & ((group & 1) == 1))
        def _():
            for copy in frame_copies((group - FAR_AT + 1) >> 1):
                copy.wait_recv()

        @pl.when((group >= NEAR_AT - 4) & (group < MATE_AT))
        def _():
            for copy in frame_copies(group - NEAR_AT + 8):
                copy.wait_recv()

        is_odd = (group & 1) == 1
        chunk = jnp.where(is_odd, 9 + ((group - 5) >> 1), 4 + ((group - 4) >> 1))
        chunk = jnp.where(group < 4, jnp.where(group == 0, 8, group), chunk)

        @pl.when(group < NEAR_AT - 1)
        def _():
            for copy in frame_copies(chunk):
                copy.start()

        @pl.when(group > FAR_AT)
        def _():
            y_copy(group - FAR_AT - 1).start()

    def turn(row, _, out, old):
        y_ref[aligned(out, COLS), aligned(row, ROWS)] = old[...].T

    def step(last, now, following, cov, cov_next, old, old_last):
        row, col, out = now
        products = covariance_pieces(all_ref, *following[:2], cov_next)
        pieces = value_pieces(cov, ln_ref, rn_ref, row, col)
        for _, (r, values) in interleave(pieces, products):
            tile[aligned(row + r, STEP), aligned(out, COLS)] = values
            old[r : r + STEP, :] = encode(values)
        turn(*last, old_last)

    first = group_place(jnp.int32(0), parity)
    for _ in covariance_pieces(all_ref, *first[:2], cov0):
        pass
    old1[...] = jnp.zeros_like(old1)

    def body(group, places):
        last, now = places
        second = second_place(group, now)
        following = group_place(jnp.minimum(group + 1, GROUPS - 1), parity)
        step(last, now, second, cov0, cov1, old0, old1)
        between(group)
        step(now, second, following, cov1, cov0, old1, old0)
        return second, following

    last, _ = lax.fori_loop(0, GROUPS, body, (first, first))
    turn(*last, old1)
    last_copy = GROUPS - FAR_AT - 1
    y_copy(jnp.int32(last_copy)).start()

    @pl.loop(0, 3 * CHUNKS)
    def _(k):
        for copy in frame_copies(k):
            copy.wait_send()

    @pl.loop(0, last_copy + 1)
    def _(k):
        y_copy(k).wait()


def main(coords, count):
    return pl.pallas_call(
        functools.partial(main_kernel, count),
        in_specs=[VMEM],
        out_specs=[VMEM] * 6,
        out_shape=[
            jax.ShapeDtypeStruct((FR, WIDTH), jnp.float32),
            jax.ShapeDtypeStruct((WIDTH, FR), jnp.bfloat16),
            jax.ShapeDtypeStruct((WIDTH - FR, FR), jnp.bfloat16),
            jax.ShapeDtypeStruct((3, FR, ATOMS), jnp.bfloat16),
            jax.ShapeDtypeStruct((FR, 128), jnp.float32),
            jax.ShapeDtypeStruct((8, 4 * FR), jnp.float32),
        ],
        scratch_shapes=[
            pltpu.VMEM((3, 4 * FR, ATOMS), jnp.bfloat16),
            pltpu.VMEM((3, 3, ROWS, COLS), jnp.float32),
            pltpu.VMEM((3, 3, ROWS, COLS), jnp.float32),
            pltpu.VMEM((ROWS, COLS), jnp.bfloat16),
            pltpu.VMEM((ROWS, COLS), jnp.bfloat16),
            pltpu.SemaphoreType.DMA((2, 3 * CHUNKS)),
            pltpu.SemaphoreType.DMA((2, 3 * CHUNKS)),
            pltpu.SemaphoreType.DMA((2, GROUPS - FAR_AT)),
        ],
        compiler_params=pltpu.CompilerParams(
            collective_id=0, has_side_effects=True, vmem_limit_bytes=MAIN_LIMIT
        ),
        cost_estimate=pl.CostEstimate(
            flops=45 * FR * FR * ATOMS, bytes_accessed=32 << 20, transcendentals=0
        ),
        name="deviations",
    )(coords)


def decode(values):
    return lax.rsqrt(lax.rsqrt(values.astype(jnp.float32)))


def finish_kernel(
    tile, y_ref, got_ref, own_ref, ln_ref, rn_ref, out_ref,
    far_tile, rest_tile, low_tile, column, turned, cov0, cov1, old0, old1, sem,
):
    parity = lax.rem(lax.axis_index("frames"), 2)
    copies = []

    def copy(source, slot, rows, cols, start=True):
        copies.append(
            pltpu.make_async_copy(source, out_ref.at[slot, rows, cols], sem.at[len(copies)])
        )
        if start:
            copies[-1].start()
        return copies[-1]

    def half(i):
        return aligned(i * HALF, HALF)

    both, last = pl.ds(0, FR), pl.ds(LAST, COLS)
    near_slot, near_flip = near_place(parity)
    mate_slot, mate_flip = mate_place(parity)
    quarters = (
        (NEAR_OUT, near_slot, near_flip, rest_tile.at[0]),
        (MATE_OUT, mate_slot, mate_flip, rest_tile.at[1]),
    )
    copy(tile.at[:, pl.ds(FAR, FR)], 4 * (1 - parity), both, both)
    for first, slot, flip, _ in quarters:
        for i in range(2):
            other = half(other_half(i, flip))
            copy(tile.at[half(i), pl.ds(first, HALF)], slot, half(i), other)
    for c in range(CHUNKS):
        rows, cols = pl.ds(0, HALF if c == CHUNKS - 1 else (c + 1) * COLS), pl.ds(c * COLS, COLS)
        copy(tile.at[rows, cols], 2, rows, cols)

    def later(source, slot, rows, cols):
        return copy(source, slot, rows, cols, start=False)

    first_rows, second_rows = pl.ds(HALF, COLS), pl.ds(LAST, COLS)
    far_copies = [later(far_tile.at[half(i)], 4 * parity, half(i), both) for i in range(2)]
    (near_copies, mate_copies) = (
        [later(tiles.at[:, half(i)], slot, half(other_half(i, 1 - flip)), half(i)) for i in range(2)]
        for _, slot, flip, tiles in quarters
    )
    completed = [
        [far_copies[0], *near_copies, later(column.at[pl.ds(0, COLS)], 2, first_rows, last)],
        [far_copies[1], *mate_copies, later(column.at[pl.ds(COLS, COLS)], 2, second_rows, last)],
    ]
    for c in range(1, CHUNKS):
        low, cols = pl.ds(c * COLS, COLS), pl.ds(0, min(c * COLS, HALF))
        completed[c > 1].append(later(low_tile.at[low, cols], 2, low, cols))
    completed[1].append(later(turned, 2, last, first_rows))

    def decode_pieces(s, piece):
        rows = aligned(s * HALF + piece * 32, 32)
        far_tile[rows, :] = decode(got_ref[rows, :])
        near_or_mate = aligned(NEAR_OUT - FAR + s * HALF + piece * 32, 32)
        rest_tile[s, pl.ds(piece * 32, 32), :] = decode(got_ref[near_or_mate, :])
        low = pl.ds(COLS + piece * 16, 16) if s == 0 else pl.ds(HALF + piece * 32, 32)
        low_tile[low, :] = decode(y_ref[low, 0:HALF])

    def step(s, cov, old, products):
        row = HALF + s * ROWS
        pieces = value_pieces(cov, ln_ref, rn_ref, row, LAST)
        for piece, (r, values) in interleave(pieces, products):
            column[s * ROWS + r : s * ROWS + r + STEP, :] = values
            old[r : r + STEP, :] = values
            decode_pieces(s, piece)

    for _ in covariance_pieces(own_ref, HALF, LAST, cov0):
        pass

    @pl.loop(0, 2)
    def _(s):
        @pl.when(s == 0)
        def _():
            step(0, cov0, old0, covariance_pieces(own_ref, LAST, LAST, cov1))

        @pl.when(s == 1)
        def _():
            step(1, cov1, old1, iter(()))
            turned[...] = old0[...].T

        for each, group in enumerate(completed):

            @pl.when(s == each)
            def _():
                for piece in group:
                    piece.start()

    for each in copies:
        each.wait()


def finish(*held):
    return pl.pallas_call(
        finish_kernel,
        in_specs=[ANY] + [VMEM] * 5,
        out_specs=ANY,
        out_shape=jax.ShapeDtypeStruct((5, FR, FR), jnp.float32),
        scratch_shapes=[
            pltpu.VMEM((FR, FR), jnp.float32),
            pltpu.VMEM((2, HALF, FR), jnp.float32),
            pltpu.VMEM((FR, HALF), jnp.float32),
            pltpu.VMEM((HALF, COLS), jnp.float32),
            pltpu.VMEM((COLS, COLS), jnp.float32),
            pltpu.VMEM((3, 3, ROWS, COLS), jnp.float32),
            pltpu.VMEM((3, 3, ROWS, COLS), jnp.float32),
            pltpu.VMEM((ROWS, COLS), jnp.float32),
            pltpu.VMEM((ROWS, COLS), jnp.float32),
            pltpu.SemaphoreType.DMA((32,)),
        ],
        compiler_params=pltpu.CompilerParams(vmem_limit_bytes=FINISH_LIMIT),
        name="finish",
    )(*held)


def on_device(coords):
    out = finish(*main(coords, lax.axis_size("frames")))
    return jnp.transpose(out, (1, 0, 2))


def solution(mesh):
    return jax.shard_map(
        on_device,
        mesh=mesh,
        in_specs=(P(None, "frames", None),),
        out_specs=P("frames", None, None),
        check_vma=False,
    )
```
